128 devices in a mesh: shot: 8 (over x, core), sub: 16 (over z, y).
Axes of the slice: x: 4, y: 4, z: 4, core: 2. Of those that a mesh axis runs over, the one named last changes fastest.
Arguments:
- wave_now: float32 [8, 256, 128, 256], P('shot', 'sub'), may hold values from -6 to 6
- wave_before: float32 [8, 256, 128, 256], P('shot', 'sub'), may hold values from -6 to 6
- courant: float32 [8, 256, 128, 256], P('shot', 'sub'), may hold values from 0.05 to 0.2
- source_waves: bfloat16 [4, 8, 256, 128, 256], P(None, 'shot', 'sub'), may hold values from -6 to 6
- tile_ids: int32 [8, 8192, 1], P('shot', 'sub'), may hold values from 0 to 127; in each aligned block of 512 rows (0 to 511, 512 to 1023, ..., all dimensions but the last counted through in order) at most 8 rows name the same one
- slot_ids: int32 [8, 8192], P('shot', 'sub'), may hold values from 0 to 15
Outputs:
- wave_last: float32 [8, 256, 128, 256], P('shot', 'sub')
- wave_prior: float32 [8, 256, 128, 256], P('shot', 'sub')
- image: float32 [128, 16, 1024], P(('shot', 'sub'))
The draws below stay inside these ranges and needn't reach their ends.
Inputs may be any that keep to these rules, and one draw needn't show every extreme that they name: `tile_ids`: among the 512 blocks of one device no tile is named more than 8 times, a bound that some block reaches; every tile is named somewhere.
All inputs are finite; a program needn't handle non-finite values.
Results may differ from the reference program's by a relative error of at most 0.0003.
Values sent between devices are 32-bit elements; how exact they have to be, the bound alone decides.
A program may use at most 128 MiB of HBM per device.

```python
import math
import jax
import jax.numpy as jnp
import numpy as np

CY = 128
CZ = 256
ITERS = 4
TSLOTS = 16
SHOTS = 8
NX = 256
NBLK = 512
BLK = 1024
TILES = 128
CAP = 8
N_SUB = 16


def place_ends(values, own_key, low, high):
    place = [jax.random.randint(jax.random.fold_in(own_key, axis), (), 0, length) for axis, length in enumerate(values.shape)]
    longest = values.shape.index(max(values.shape))
    beside = place[:longest] + [(place[longest] + 1) % values.shape[longest]] + place[longest + 1:]
    return values.at[tuple(place)].set(low).at[tuple(beside)].set(high)


def level_of(stream_key, dims, shards, low, top_value):
    def one(axis_at, blocks):
        steps = jax.random.uniform(jax.random.fold_in(jax.random.fold_in(stream_key, 6), axis_at), (blocks,), jnp.float32, low / len(shards), top_value / len(shards))
        return jnp.repeat(jnp.exp(steps), dims[axis_at] // blocks).reshape((-1,) + (1,) * (len(dims) - axis_at - 1))

    loudness = one(*shards[0])
    for cut in shards[1:]:
        loudness = loudness * one(*cut)
    return loudness


def deal_out(key, own, number, rows, amount, top, bound, skew):
    sequence = jax.random.permutation(key, amount)
    packed, common = shares(amount, rows * top, bound, skew, True), shares(amount, rows * top, bound, skew, False)
    places = jnp.arange(amount)

    def named(lengths, rotation):
        used = int((lengths > 0).sum())
        fixed = max(1, used // 4)
        shifted = fixed + (places - fixed + rotation * (used - fixed)) % max(1, amount - fixed)
        return jnp.zeros((amount,), jnp.int32).at[sequence[jnp.where(places < fixed, places, shifted)]].set(jnp.asarray(lengths, jnp.int32))

    lengths = jnp.where(number % 4 == 0, named(packed, number // 4), named(common, number - number // 4 - 1))
    mixed = jax.random.permutation(jax.random.fold_in(own, 3), amount)
    donor, sink = mixed[0:amount // 2 * 2:2], mixed[1:amount // 2 * 2:2]
    slack = jnp.minimum(lengths[donor] - 1, bound - lengths[sink]) // 2
    slack = jnp.where((donor == sequence[0]) | (sink == sequence[0]) | (lengths[sink] == 0), 0, jnp.maximum(slack, 0))
    shifted = jax.random.randint(jax.random.fold_in(own, 4), (amount // 2,), 0, 1 << 20) % (slack + 1)
    lengths = lengths.at[donor].add(-shifted).at[sink].add(shifted)
    labels = jnp.searchsorted(jnp.cumsum(lengths), jnp.arange(rows * top), side="right").astype(jnp.int32)
    table = labels.reshape(top, rows).T
    table = table[jax.random.permutation(jax.random.fold_in(own, 1), rows)]
    rotation = jax.random.randint(jax.random.fold_in(own, 2), (rows, 1), 0, top)
    return jnp.take_along_axis(table, (jnp.arange(top)[None, :] + rotation) % top, axis=1)


def shares(number_of, total, bound, lean, full):
    portions = [(1 << 20) // math.isqrt(standing ** lean) + 1 for standing in range(1, number_of + 1)]
    largest = bound if full else min(bound, max(-(-total // number_of), total * portions[0] // sum(portions)))
    least = 1 if total - largest >= number_of - 1 else 0
    given, rest = [largest] + [least] * (number_of - 1), total - largest - least * (number_of - 1)
    while rest > 0:
        free = [i for i in range(1, number_of) if given[i] < largest] or [i for i in range(1, number_of) if given[i] < bound]
        pool, budget = sum([portions[i] for i in free]), rest
        for i in free:
            extra = min(bound - given[i], max(1, budget * portions[i] // pool), rest)
            given[i] = given[i] + extra
            rest = rest - extra
    return np.array(given)


def noise(key, dims, spread, most, pieces=(), held_as=jnp.bfloat16):
    array = jax.random.normal(key, dims, jnp.float32) * spread
    if len(pieces) > 0:
        array = level_of(key, dims, pieces, -0.22, 0.18) * array
    return jnp.clip(array, min=-most, max=most).astype(held_as)


def setup_inputs(seed: int = 0) -> dict:
    streams_of = jax.random.split(jax.random.key(seed), 7)
    wave_now = noise(streams_of[0], (SHOTS, NX, CY, CZ), 1.0, 6.0, ((0, 8), (1, 16)), jnp.float32)
    wave_before = noise(streams_of[1], (SHOTS, NX, CY, CZ), 1.0, 6.0, ((0, 8), (1, 16)), jnp.float32)
    courant = jnp.clip(jnp.exp(math.log(0.2) - 1.3862944 * jax.random.uniform(streams_of[2], (SHOTS, NX, CY, CZ), jnp.float32) ** level_of(streams_of[2], (SHOTS, NX, CY, CZ), ((0, 8), (1, 16)), -0.2, 0.2)), 0.05, 0.2)
    source_waves = noise(streams_of[3], (ITERS, SHOTS, NX, CY, CZ), 1.0, 6.0, ((1, 8), (2, 16)))
    tile_ids_keys = jax.random.split(jax.random.fold_in(streams_of[4], 1), SHOTS * (N_SUB * NBLK) // NBLK)
    tile_ids_turns = jax.random.permutation(jax.random.fold_in(streams_of[4], 3), SHOTS * (N_SUB * NBLK) // NBLK)
    tile_ids = jax.vmap(lambda own, number: deal_out(jax.random.fold_in(streams_of[4], 2), own, number, NBLK, TILES, 1, CAP, 2))(tile_ids_keys, tile_ids_turns).reshape((SHOTS, N_SUB * NBLK, 1))
    slot_ids = place_ends(jax.random.randint(streams_of[5], (SHOTS, N_SUB * NBLK), 0, TSLOTS), jax.random.fold_in(streams_of[5], 1), 0, TSLOTS - 1).astype(jnp.int32)
    return {"wave_now": wave_now, "wave_before": wave_before, "courant": courant, "source_waves": source_waves, "tile_ids": tile_ids, "slot_ids": slot_ids}


fd_weights = (-205.0 / 72.0, 8.0 / 5.0, -1.0 / 5.0, 8.0 / 315.0, -1.0 / 560.0)


def laplace(field):
    length = field.shape[-3]
    width_y = field.shape[-2]
    width_z = field.shape[-1]
    core = field[..., 4:length - 4, :, :]
    padded = jnp.pad(core, [(0, 0)] * (core.ndim - 2) + [(4, 4), (4, 4)])
    total = 3.0 * fd_weights[0] * core
    for k in range(1, 5):
        total = total + fd_weights[k] * (field[..., 4 + k:length - 4 + k, :, :] + field[..., 4 - k:length - 4 - k, :, :])
        total = total + fd_weights[k] * (padded[..., 4 + k:4 + k + width_y, 4:4 + width_z] + padded[..., 4 - k:4 - k + width_y, 4:4 + width_z])
        total = total + fd_weights[k] * (padded[..., 4:4 + width_y, 4 + k:4 + k + width_z] + padded[..., 4:4 + width_y, 4 - k:4 - k + width_z])
    return total


def reference(wave_now, wave_before, courant, source_waves, tile_ids, slot_ids):
    current = wave_now
    before = wave_before
    partial_value = jnp.zeros_like(wave_now)
    for step in range(ITERS):
        padded = jnp.pad(current, ((0, 0), (4, 4), (0, 0), (0, 0)))
        after = 2.0 * current - before + courant * laplace(padded)
        before = current
        current = after
        partial_value = partial_value + source_waves[step].astype(jnp.float32) * current
    blocks = partial_value.reshape(SHOTS * N_SUB * NBLK, BLK)
    keys = (tile_ids.reshape(-1) * TSLOTS + slot_ids.reshape(-1)).astype(jnp.int32)
    image = jax.ops.segment_sum(blocks, keys, num_segments=TILES * TSLOTS)
    return current, before, image.reshape(TILES, TSLOTS, BLK)
```

```python
import jax
import jax.numpy as jnp
from jax import lax
from jax.experimental import pallas as pl
from jax.experimental.pallas import tpu as pltpu
from jax.sharding import PartitionSpec as P

ITERS = 4
BY = 4
TSLOTS = 16
MESH = pl.DeviceIdType.MESH
W = (-205.0 / 72.0, 8.0 / 5.0, -1.0 / 5.0, 8.0 / 315.0, -1.0 / 560.0)

NX, CY, CZ = 16, 128, 256
ROWS = 16
CHUNKS = CY // ROWS
PAD = 8
MIB = 1024 * 1024


def bf(v):
    return v.astype(jnp.bfloat16)


def f32(v):
    return v.astype(jnp.float32)


def steps_kernel(now, before, courant, source, last, prior, image, wave, speed, src, part, zpart, band, load, send, recv, store):
    sub = lax.axis_index("sub")
    count = lax.axis_size("sub")
    has_left = sub > 0
    has_right = sub < count - 1
    left = {"sub": jnp.maximum(sub - 1, 0)}
    right = {"sub": jnp.minimum(sub + 1, count - 1)}

    inner = (pl.ds(4, NX), pl.ds(PAD, CY))
    loads = [
        pltpu.make_async_copy(now.at[0], wave.at[(0, *inner)], load.at[0]),
        pltpu.make_async_copy(before.at[0], wave.at[(1, *inner)], load.at[1]),
        pltpu.make_async_copy(courant.at[0], speed, load.at[2]),
    ]
    loads += [pltpu.make_async_copy(source.at[t, 0], src.at[t], load.at[3 + t]) for t in range(ITERS)]
    for copy in loads:
        copy.start()

    barrier = pltpu.get_barrier_semaphore()

    @pl.when(has_left)
    def _():
        pl.semaphore_signal(barrier, inc=1, device_id=left, device_id_type=MESH)

    @pl.when(has_right)
    def _():
        pl.semaphore_signal(barrier, inc=1, device_id=right, device_id_type=MESH)

    edge = jnp.zeros((2, 4, CY, CZ), jnp.float32)

    @pl.when(jnp.logical_not(has_left))
    def _():
        wave[:, 0:4, PAD : PAD + CY, :] = edge

    @pl.when(jnp.logical_not(has_right))
    def _():
        wave[:, NX + 4 : NX + 8, PAD : PAD + CY, :] = edge

    strip = jnp.zeros((2, NX, PAD, CZ), jnp.float32)
    wave[:, 4 : NX + 4, 0:PAD, :] = strip
    wave[:, 4 : NX + 4, PAD + CY :, :] = strip
    gap = jnp.abs(lax.broadcasted_iota(jnp.int32, (CZ, CZ), 0) - lax.broadcasted_iota(jnp.int32, (CZ, CZ), 1))
    taps = jnp.zeros((CZ, CZ), jnp.float32)
    for k in range(1, 5):
        taps = jnp.where(gap == k, W[k], taps)
    band[0] = bf(taps)
    band[1] = bf(taps - f32(bf(taps)))

    pl.semaphore_wait(barrier, jnp.where(has_left, 1, 0) + jnp.where(has_right, 1, 0))

    def to_left(t, j, source_ref=None):
        b = lax.rem(t, 2)
        rows = pl.ds(PAD + j * ROWS, ROWS)
        return pltpu.make_async_remote_copy(
            src_ref=source_ref if source_ref is not None else wave.at[b, pl.ds(4, 4), rows],
            dst_ref=wave.at[b, pl.ds(NX + 4, 4), rows],
            send_sem=send.at[0, t, j],
            recv_sem=recv.at[0, t, j],
            device_id=left,
            device_id_type=MESH,
        )

    def to_right(t, j, source_ref=None):
        b = lax.rem(t, 2)
        rows = pl.ds(PAD + j * ROWS, ROWS)
        return pltpu.make_async_remote_copy(
            src_ref=source_ref if source_ref is not None else wave.at[b, pl.ds(NX, 4), rows],
            dst_ref=wave.at[b, pl.ds(0, 4), rows],
            send_sem=send.at[1, t, j],
            recv_sem=recv.at[1, t, j],
            device_id=right,
            device_id_type=MESH,
        )

    def first(j, _):
        rows = pl.ds(j * ROWS, ROWS)

        @pl.when(has_left)
        def _():
            to_left(0, j, now.at[0, pl.ds(0, 4), rows]).start()

        @pl.when(has_right)
        def _():
            to_right(0, j, now.at[0, pl.ds(NX - 4, 4), rows]).start()

        return 0

    lax.fori_loop(0, CHUNKS, first, 0)

    for copy in loads[:3]:
        copy.wait()

    def chunk(t, j):
        cur = lax.rem(t, 2)
        nxt = 1 - cur
        row0 = j * ROWS
        rows = pl.ds(pl.multiple_of(PAD + row0, 8), ROWS)
        plain = pl.ds(pl.multiple_of(row0, ROWS), ROWS)

        v = wave[cur, pl.ds(4, NX), rows, :].reshape(NX * ROWS, CZ)
        hi = bf(v)
        lo = bf(v - f32(hi))
        z = jnp.dot(hi, band[0], preferred_element_type=jnp.float32)
        z += jnp.dot(lo, band[0], preferred_element_type=jnp.float32)
        z += jnp.dot(hi, band[1], preferred_element_type=jnp.float32)
        zpart[...] = z.reshape(NX, ROWS, CZ)

        @pl.when(has_left)
        def _():
            to_right(t, j).wait_recv()

            @pl.when(t > 0)
            def _():
                to_left(t, j).wait_send()

        @pl.when(has_right)
        def _():
            to_left(t, j).wait_recv()

            @pl.when(t > 0)
            def _():
                to_right(t, j).wait_send()

        def layer(x, _):
            wide = wave[cur, x + 4, pl.ds(pl.multiple_of(row0, 8), ROWS + 2 * PAD), :]
            center = wide[PAD : PAD + ROWS]
            lap = 3.0 * W[0] * center + zpart[x]
            for k in range(1, 5):
                pair = wave[cur, x + 4 + k, rows, :] + wave[cur, x + 4 - k, rows, :]
                pair += wide[PAD + k : PAD + k + ROWS] + wide[PAD - k : PAD - k + ROWS]
                lap += W[k] * pair
            after = 2.0 * center - wave[nxt, x + 4, rows, :] + speed[x, plain, :] * lap
            wave[nxt, x + 4, rows, :] = after
            term = f32(src[t, x, plain, :]) * after
            part[x, plain, :] = jnp.where(t == 0, term, part[x, plain, :] + term)
            return 0

        lax.fori_loop(0, NX, layer, 0)

        @pl.when(t < ITERS - 1)
        def _():
            @pl.when(has_left)
            def _():
                to_left(t + 1, j).start()

            @pl.when(has_right)
            def _():
                to_right(t + 1, j).start()

    def last_copies(j):
        rows = pl.ds(pl.multiple_of(PAD + j * ROWS, 8), ROWS)
        plain = pl.ds(pl.multiple_of(j * ROWS, ROWS), ROWS)
        final = ITERS % 2
        return (
            pltpu.make_async_copy(wave.at[final, pl.ds(4, NX), rows], last.at[0, :, plain], store.at[0, j]),
            pltpu.make_async_copy(part.at[:, plain], image.at[:, plain], store.at[1, j]),
        )

    prior_copy = pltpu.make_async_copy(wave.at[((ITERS + 1) % 2, *inner)], prior.at[0], store.at[2, 0])

    def one_step(t, _):
        for s in range(ITERS):

            @pl.when(t == s)
            def _():
                loads[3 + s].wait()

        @pl.when(t == ITERS - 1)
        def _():
            prior_copy.start()

        def one_chunk(j, _):
            chunk(t, j)

            @pl.when(t == ITERS - 1)
            def _():
                for copy in last_copies(j):
                    copy.start()

            return 0

        lax.fori_loop(0, CHUNKS, one_chunk, 0)
        return 0

    lax.fori_loop(0, ITERS, one_step, 0)

    def finish(j, _):
        for copy in last_copies(j):
            copy.wait()
        rows = pl.ds(j * ROWS, ROWS)

        @pl.when(has_left)
        def _():
            to_left(0, j, now.at[0, pl.ds(0, 4), rows]).wait_send()

        @pl.when(has_right)
        def _():
            to_right(0, j, now.at[0, pl.ds(NX - 4, 4), rows]).wait_send()

        return 0

    lax.fori_loop(0, CHUNKS, finish, 0)
    prior_copy.wait()


def run_steps(now, before, courant, source):
    field = jax.ShapeDtypeStruct((1, NX, CY, CZ), jnp.float32)
    return pl.pallas_call(
        steps_kernel,
        out_shape=(field, field, jax.ShapeDtypeStruct((NX, CY, CZ), jnp.float32)),
        in_specs=[pl.BlockSpec(memory_space=pl.ANY)] * 4,
        out_specs=(pl.BlockSpec(memory_space=pl.ANY),) * 3,
        scratch_shapes=[
            pltpu.VMEM((2, NX + 8, CY + 2 * PAD, CZ), jnp.float32),
            pltpu.VMEM((NX, CY, CZ), jnp.float32),
            pltpu.VMEM((ITERS, NX, CY, CZ), jnp.bfloat16),
            pltpu.VMEM((NX, CY, CZ), jnp.float32),
            pltpu.VMEM((NX, ROWS, CZ), jnp.float32),
            pltpu.VMEM((2, CZ, CZ), jnp.bfloat16),
            pltpu.SemaphoreType.DMA((3 + ITERS,)),
            pltpu.SemaphoreType.DMA((2, ITERS, CHUNKS)),
            pltpu.SemaphoreType.DMA((2, ITERS, CHUNKS)),
            pltpu.SemaphoreType.DMA((3, CHUNKS)),
        ],
        compiler_params=pltpu.CompilerParams(collective_id=0, has_side_effects=True, vmem_limit_bytes=60 * MIB),
        cost_estimate=pl.CostEstimate(flops=400_000_000, bytes_accessed=16_000_000, transcendentals=0),
    )(now, before, courant, source)


PARTS = ((0, 384), (384, 384), (768, 256))
ORDERS = ((0, 1, 2), (1, 2, 0), (2, 0, 1))
STRIDES = (32, 4, 1)
NBLK = 512


def image_kernel(blocks, keys, out, mine, other, other_keys, halves, *rest):
    shot = lax.axis_index("shot")
    sub = lax.axis_index("sub")
    core = lax.rem(shot, 2)
    place = (shot // 2, sub // 4, lax.rem(sub, 4))
    dense, got, (swap, send, recv) = rest[:3], (rest[3:6], rest[6:9], rest[9:12]), rest[12:]

    def at(x, z, y, c):
        return (x * 2 + c, z * 4 + y)

    def beside(axis, by):
        there = list(place)
        there[axis] = lax.rem(there[axis] + by, 4)
        return at(*there, core)

    partner = at(*place, 1 - core)
    barrier = pltpu.get_barrier_semaphore()
    for device in [partner] + [beside(axis, by) for axis in range(3) for by in (1, 3)]:
        pl.semaphore_signal(barrier, inc=1, device_id=device, device_id_type=MESH)
    pl.semaphore_wait(barrier, 7)

    swaps = [
        pltpu.make_async_remote_copy(
            src_ref=blocks, dst_ref=other, send_sem=swap.at[0], recv_sem=swap.at[1], device_id=partner, device_id_type=MESH
        ),
        pltpu.make_async_remote_copy(
            src_ref=keys, dst_ref=other_keys, send_sem=swap.at[2], recv_sem=swap.at[3], device_id=partner, device_id_type=MESH
        ),
    ]
    own = pltpu.make_async_copy(blocks, mine, swap.at[4])
    for copy in swaps:
        copy.start()
    own.start()
    own.wait()

    def split(ref, base):
        def body(i, _):
            rows = pl.ds(pl.multiple_of(i * 32, 32), 32)
            v = ref[rows, :]
            hi = bf(v)
            there = pl.ds(pl.multiple_of(base + i * 32, 32), 32)
            halves[0, there, :] = hi
            halves[1, there, :] = bf(v - f32(hi))
            return 0

        lax.fori_loop(0, NBLK // 32, body, 0)

    split(mine, 0)
    for copy in swaps:
        copy.wait_recv()
    split(other, NBLK)

    row = lax.broadcasted_iota(jnp.int32, (256, 1), 0)

    def group(p, dest):
        a1, a2, a3 = ORDERS[p]
        tile = dest * STRIDES[a1] + (row // 64) * STRIDES[a2] + lax.rem(row // 16, 4) * STRIDES[a3] + core * 16
        key = tile * TSLOTS + lax.rem(row, 16)
        first, lanes = PARTS[p]
        total = jnp.zeros((256, lanes), jnp.float32)
        for side, named in enumerate((keys, other_keys)):
            pick = bf(f32(key == named[0:1, :]))
            for half in range(2):
                total += jnp.dot(
                    pick,
                    halves[half, side * NBLK : (side + 1) * NBLK, first : first + lanes],
                    preferred_element_type=jnp.float32,
                )
        dense[p][dest] = total.reshape(4, 4, 16, lanes)

    def reduced(p, stage):
        return tuple(place[axis] for axis in ORDERS[p][:stage])

    def half_of(stage, front):
        size = 8 if stage == 2 else 2
        return pl.ds(0 if front else size, size)

    def message(p, stage, kind):
        axis = ORDERS[p][stage]
        by = 1 if kind < 3 else 3
        dest = lax.rem(place[axis] + (2 if kind % 3 == 0 else by), 4)
        return pltpu.make_async_remote_copy(
            src_ref=dense[p].at[(*reduced(p, stage), dest, half_of(stage, kind in (0, 2, 4)))],
            dst_ref=got[p][stage].at[kind],
            send_sem=send.at[p, stage, kind],
            recv_sem=recv.at[p, stage, kind],
            device_id=beside(axis, by),
            device_id_type=MESH,
        )

    def add(p, stage, dest, front, kind):
        where = (*reduced(p, stage), dest, half_of(stage, front))
        dense[p][where] = dense[p][where] + got[p][stage][kind]

    def toward(p, stage, by):
        return lax.rem(place[ORDERS[p][stage]] + by, 4)

    for stage in range(3):
        for p in range(3):
            if stage == 0:
                group(p, toward(p, stage, 2))
            message(p, stage, 0).start()
            message(p, stage, 3).start()
        for p in range(3):
            if stage == 0:
                group(p, toward(p, stage, 1))
            message(p, stage, 1).start()
            if stage == 0:
                group(p, toward(p, stage, 3))
            message(p, stage, 4).start()
        for p in range(3):
            message(p, stage, 0).wait_recv()
            add(p, stage, toward(p, stage, 1), True, 0)
            message(p, stage, 2).start()
            message(p, stage, 3).wait_recv()
            add(p, stage, toward(p, stage, 3), False, 3)
            message(p, stage, 5).start()
        for p in range(3):
            if stage == 0:
                group(p, toward(p, stage, 0))
        for p in range(3):
            for kind in (1, 4, 2, 5):
                message(p, stage, kind).wait_recv()
                add(p, stage, toward(p, stage, 0), kind in (2, 4), kind)
    for p in range(3):
        first, lanes = PARTS[p]
        out[0, :, first : first + lanes] = dense[p][reduced(p, 3)]
    for stage in range(3):
        for p in range(3):
            for kind in range(6):
                message(p, stage, kind).wait_send()
    for copy in swaps:
        copy.wait_send()


def run_image(blocks, keys):
    dense = [pltpu.VMEM((4, 4, 4, TSLOTS, lanes), jnp.float32) for _, lanes in PARTS]
    got = []
    for _, lanes in PARTS:
        got += [
            pltpu.VMEM((6, 2, 4, TSLOTS, lanes), jnp.float32),
            pltpu.VMEM((6, 2, TSLOTS, lanes), jnp.float32),
            pltpu.VMEM((6, TSLOTS // 2, lanes), jnp.float32),
        ]
    block = BY * CZ
    return pl.pallas_call(
        image_kernel,
        out_shape=jax.ShapeDtypeStruct((1, TSLOTS, block), jnp.float32),
        in_specs=[pl.BlockSpec(memory_space=pl.ANY), pl.BlockSpec(memory_space=pltpu.VMEM)],
        out_specs=pl.BlockSpec(memory_space=pltpu.VMEM),
        scratch_shapes=[
            pltpu.VMEM((NBLK, block), jnp.float32),
            pltpu.VMEM((NBLK, block), jnp.float32),
            pltpu.VMEM((8, NBLK), jnp.int32),
            pltpu.VMEM((2, 2 * NBLK, block), jnp.bfloat16),
            *dense,
            *got,
            pltpu.SemaphoreType.DMA((5,)),
            pltpu.SemaphoreType.DMA((3, 3, 6)),
            pltpu.SemaphoreType.DMA((3, 3, 6)),
        ],
        compiler_params=pltpu.CompilerParams(collective_id=1, has_side_effects=True, vmem_limit_bytes=60 * MIB),
        cost_estimate=pl.CostEstimate(flops=4_000_000_000, bytes_accessed=4_000_000, transcendentals=0),
    )(blocks, keys)


def on_device(wave_now, wave_before, courant, source_waves, tile_ids, slot_ids):
    last, prior, partial = run_steps(wave_now, wave_before, courant, source_waves)
    keys = tile_ids.reshape(1, NBLK) * TSLOTS + slot_ids.reshape(1, NBLK)
    keys = jnp.broadcast_to(keys, (8, NBLK))
    return last, prior, run_image(partial.reshape(NBLK, BY * CZ), keys)


def solution(mesh):
    return jax.shard_map(
        on_device,
        mesh=mesh,
        in_specs=(
            P("shot", "sub"),
            P("shot", "sub"),
            P("shot", "sub"),
            P(None, "shot", "sub"),
            P("shot", "sub", None),
            P("shot", "sub"),
        ),
        out_specs=(
            P("shot", "sub"),
            P("shot", "sub"),
            P(("shot", "sub")),
        ),
        check_vma=False,
    )
```

```python
import jax
import jax.numpy as jnp
from jax import lax
from jax.experimental import pallas as pl
from jax.experimental.pallas import tpu as pltpu
from jax.sharding import PartitionSpec as P

ITERS = 4
BY = 4
TSLOTS = 16
MESH = pl.DeviceIdType.MESH
W = (-205.0 / 72.0, 8.0 / 5.0, -1.0 / 5.0, 8.0 / 315.0, -1.0 / 560.0)

NX, CY, CZ = 16, 128, 256
ROWS = 16
CHUNKS = CY // ROWS
PAD = 8
MIB = 1024 * 1024
STEP_BLOCKS = NX * ROWS // BY
LANES = 128
NBLK = NX * CY // BY
XB = 2
GROUP = 8
WIDE = ROWS + 2 * PAD
INNER, OUTER = (4, 8), (0, 12)
PARTS = ((0, 3), (3, 3), (6, 2))
ORDERS = ((0, 1, 2), (1, 2, 0), (2, 0, 1))


def bf(v):
    return v.astype(jnp.bfloat16)


def f32(v):
    return v.astype(jnp.float32)


def kernel(now, before, courant, source, tiles_here, slots_here, last, prior, out, wave, speed, src, part, other, zpart, band, across, keys, other_keys, rhs, dense, *rest):
    ring, direct, final, (load, send, recv, store, swap, post, mail) = rest[0:3], rest[3:6], rest[6:9], rest[9:]
    shot = lax.axis_index("shot")
    sub = lax.axis_index("sub")
    count = lax.axis_size("sub")
    core = lax.rem(shot, 2)
    place = (shot // 2, sub // 4, lax.rem(sub, 4))
    has_left = sub > 0
    has_right = sub < count - 1
    left = (shot, jnp.maximum(sub - 1, 0))
    right = (shot, jnp.minimum(sub + 1, count - 1))

    def beside(axis, by):
        x, z, y = (lax.rem(c + by, 4) if a == axis else c for a, c in enumerate(place))
        return (x * 2 + core, z * 4 + y)

    partner = (shot + 1 - 2 * core, sub)

    inner = (pl.ds(4, NX), pl.ds(PAD, CY))
    loads = [
        pltpu.make_async_copy(now.at[0], wave.at[(0, *inner)], load.at[0]),
        pltpu.make_async_copy(before.at[0], wave.at[(1, *inner)], load.at[1]),
        pltpu.make_async_copy(courant.at[0], speed, load.at[2]),
    ]
    loads += [pltpu.make_async_copy(source.at[t, 0], src.at[t], load.at[3 + t]) for t in range(ITERS)]
    for copy in loads:
        copy.start()

    barrier = pltpu.get_barrier_semaphore()

    @pl.when(has_left)
    def _():
        pl.semaphore_signal(barrier, inc=1, device_id=left, device_id_type=MESH)

    @pl.when(has_right)
    def _():
        pl.semaphore_signal(barrier, inc=1, device_id=right, device_id_type=MESH)

    for device in [partner] + [beside(axis, by) for axis in range(3) for by in (1, 2, 3)]:
        pl.semaphore_signal(barrier, inc=1, device_id=device, device_id_type=MESH)

    edge = jnp.zeros((2, 4, CY, CZ), jnp.float32)

    @pl.when(jnp.logical_not(has_left))
    def _():
        wave[:, 0:4, PAD : PAD + CY, :] = edge

    @pl.when(jnp.logical_not(has_right))
    def _():
        wave[:, NX + 4 : NX + 8, PAD : PAD + CY, :] = edge

    strip = jnp.zeros((2, NX, PAD, CZ), jnp.float32)
    wave[:, 4 : NX + 4, 0:PAD, :] = strip
    wave[:, 4 : NX + 4, PAD + CY :, :] = strip
    def taps(gap):
        weights = jnp.zeros(gap.shape, jnp.float32)
        for k in range(1, 5):
            weights = jnp.where(gap == k, W[k] / W[1], weights)
        return weights

    def grid(shape, axis):
        return lax.broadcasted_iota(jnp.int32, shape, axis)

    band[...] = bf(taps(jnp.abs(grid((CZ, CZ), 0) - grid((CZ, CZ), 1))))
    shape = (GROUP * ROWS, GROUP * WIDE)
    gap = jnp.abs(lax.rem(grid(shape, 0), ROWS) + PAD - lax.rem(grid(shape, 1), WIDE))
    across[...] = bf(jnp.where(grid(shape, 0) // ROWS == grid(shape, 1) // WIDE, taps(gap), 0.0))

    at_block = lax.broadcasted_iota(jnp.int32, (1, NBLK), 1)
    at_chunk = lax.broadcasted_iota(jnp.int32, (CHUNKS, NBLK), 0)
    spread = bf(
        f32(
            lax.rem(lax.broadcasted_iota(jnp.int32, (NBLK, LANES), 1), STEP_BLOCKS)
            == lax.broadcasted_iota(jnp.int32, (NBLK, LANES), 0) // (CY // BY) * (ROWS // BY)
            + lax.rem(lax.broadcasted_iota(jnp.int32, (NBLK, LANES), 0), ROWS // BY)
        )
    )
    in_chunk = lax.rem(at_block // (ROWS // BY), CHUNKS) == at_chunk
    named_tile, named_slot = (
        jnp.dot(bf(jnp.where(in_chunk, f32(ref[...]), 0.0)), spread, preferred_element_type=jnp.float32)
        for ref in (tiles_here, slots_here)
    )
    keys[...] = named_tile * TSLOTS + named_slot

    pl.semaphore_wait(barrier, jnp.where(has_left, 1, 0) + jnp.where(has_right, 1, 0) + 10)

    def to_left(t, j, source_ref=None):
        b = lax.rem(t, 2)
        rows = pl.ds(PAD + j * ROWS, ROWS)
        return pltpu.make_async_remote_copy(
            src_ref=source_ref if source_ref is not None else wave.at[b, pl.ds(4, 4), rows],
            dst_ref=wave.at[b, pl.ds(NX + 4, 4), rows],
            send_sem=send.at[0, t, j],
            recv_sem=recv.at[0, t, j],
            device_id=left,
            device_id_type=MESH,
        )

    def to_right(t, j, source_ref=None):
        b = lax.rem(t, 2)
        rows = pl.ds(PAD + j * ROWS, ROWS)
        return pltpu.make_async_remote_copy(
            src_ref=source_ref if source_ref is not None else wave.at[b, pl.ds(NX, 4), rows],
            dst_ref=wave.at[b, pl.ds(0, 4), rows],
            send_sem=send.at[1, t, j],
            recv_sem=recv.at[1, t, j],
            device_id=right,
            device_id_type=MESH,
        )

    def first(j, _):
        rows = pl.ds(j * ROWS, ROWS)

        @pl.when(has_left)
        def _():
            to_left(0, j, now.at[0, pl.ds(0, 4), rows]).start()

        @pl.when(has_right)
        def _():
            to_right(0, j, now.at[0, pl.ds(NX - 4, 4), rows]).start()

        return 0

    lax.fori_loop(0, CHUNKS, first, 0)

    key_swap = pltpu.make_async_remote_copy(
        src_ref=keys, dst_ref=other_keys, send_sem=swap.at[0, CHUNKS], recv_sem=swap.at[1, CHUNKS], device_id=partner, device_id_type=MESH
    )
    key_swap.start()
    dense[...] = jnp.zeros_like(dense)
    part[...] = jnp.zeros_like(part)

    for copy in loads[:3]:
        copy.wait()

    def group(t, j, places):
        cur = lax.rem(t, 2)
        nxt = 1 - cur
        window = pl.ds(pl.multiple_of(j * ROWS, ROWS), WIDE)
        rows = pl.ds(pl.multiple_of(PAD + j * ROWS, 8), ROWS)
        plain = pl.ds(pl.multiple_of(j * ROWS, ROWS), ROWS)

        v = jnp.concatenate([wave[cur, 4 + a : 8 + a, window, :] for a in places], axis=0).reshape(GROUP * WIDE, CZ)
        hi = bf(v)
        lo = bf(v - f32(hi))
        deep = jnp.dot(hi, band[...], preferred_element_type=jnp.float32)
        deep += jnp.dot(lo, band[...], preferred_element_type=jnp.float32)
        flat = jnp.dot(across[...], hi, preferred_element_type=jnp.float32)
        flat += jnp.dot(across[...], lo, preferred_element_type=jnp.float32)
        zpart[...] = deep.reshape(GROUP, WIDE, CZ)[:, PAD : PAD + ROWS] + flat.reshape(GROUP, ROWS, CZ)

        for i in range(0, GROUP, XB):
            x = places[i // 4] + i % 4
            here = slice(x, x + XB)
            center = wave[cur, x + 4 : x + 4 + XB, rows, :]
            lap = 3.0 * W[0] / W[1] * center + zpart[i : i + XB]
            for k in range(1, 5):
                pair = wave[cur, x + 4 + k : x + 4 + k + XB, rows, :] + wave[cur, x + 4 - k : x + 4 - k + XB, rows, :]
                lap += pair if k == 1 else W[k] / W[1] * pair
            after = 2.0 * center - wave[nxt, x + 4 : x + 4 + XB, rows, :] + W[1] * speed[here, plain, :] * lap
            wave[nxt, x + 4 : x + 4 + XB, rows, :] = after
            term = (f32(src[t, here, plain, :]) * after).reshape(XB * ROWS, CZ)
            there = slice(x * ROWS, (x + XB) * ROWS)
            for h in range(CZ // LANES):
                piece = term[:, h * LANES : (h + 1) * LANES]
                part[j, h, there, :] = part[j, h, there, :] + piece

    def edges(t, j):
        @pl.when(has_left)
        def _():
            to_right(t, j).wait_recv()

            @pl.when(t > 0)
            def _():
                to_left(t, j).wait_send()

        @pl.when(has_right)
        def _():
            to_left(t, j).wait_recv()

            @pl.when(t > 0)
            def _():
                to_right(t, j).wait_send()

        group(t, j, OUTER)

        @pl.when(t < ITERS - 1)
        def _():
            @pl.when(has_left)
            def _():
                to_left(t + 1, j).start()

            @pl.when(has_right)
            def _():
                to_right(t + 1, j).start()

    def last_copy(j):
        rows = pl.ds(pl.multiple_of(PAD + j * ROWS, 8), ROWS)
        plain = pl.ds(pl.multiple_of(j * ROWS, ROWS), ROWS)
        return pltpu.make_async_copy(wave.at[ITERS % 2, pl.ds(4, NX), rows], last.at[0, :, plain], store.at[j])

    prior_copy = pltpu.make_async_copy(wave.at[((ITERS + 1) % 2, *inner)], prior.at[0], store.at[CHUNKS])

    def give(j):
        return pltpu.make_async_remote_copy(
            src_ref=part.at[j], dst_ref=other.at[j], send_sem=swap.at[0, j], recv_sem=swap.at[1, j], device_id=partner, device_id_type=MESH
        )

    slot_row = f32(lax.broadcasted_iota(jnp.int32, (256, 1), 0))
    lane = lax.broadcasted_iota(jnp.int32, (1, LANES), 1)

    def fold(j):
        give(j).wait_recv()
        for r in range(BY):
            for h in range(CZ // LANES):
                both = jnp.concatenate(
                    [ref[j, h, pl.ds(r, STEP_BLOCKS, stride=BY), :] for ref in (part, other)], axis=0
                )
                hi = bf(both)
                rhs[r, 0:LANES, h * LANES : (h + 1) * LANES] = hi
                rhs[r, LANES : 2 * LANES, h * LANES : (h + 1) * LANES] = bf(both - f32(hi))
        named = jnp.where(lane < STEP_BLOCKS, keys[pl.ds(j, 1), :], other_keys[pl.ds(j, 1), :])
        named = jnp.concatenate([named, named], axis=1)

        def tiles(x, _):
            pick = bf(f32(named - f32(x * 512 + core * 256) == slot_row))
            for r in range(BY):
                sums = jnp.dot(pick, rhs[r], preferred_element_type=jnp.float32)
                for h in range(CZ // LANES):
                    tile = CZ // LANES * r + h
                    dense[tile, x] += sums[:, h * LANES : (h + 1) * LANES].reshape(4, 4, TSLOTS, LANES)
            return 0

        lax.fori_loop(0, 4, tiles, 0)

    def one_step(t, _):
        for s in range(ITERS - 1):

            @pl.when(t == s)
            def _():
                loads[3 + s].wait()

        def one_chunk(j, _):
            group(t, j, INNER)
            edges(t, j)

            @pl.when(jnp.logical_and(t == ITERS - 2, j > 0))
            def _():
                group(ITERS - 1, j - 1, INNER)

            return 0

        lax.fori_loop(0, CHUNKS, one_chunk, 0)
        return 0

    loads[2 + ITERS].wait()
    lax.fori_loop(0, ITERS - 1, one_step, 0)
    prior_copy.start()
    group(ITERS - 1, CHUNKS - 1, INNER)
    key_swap.wait_recv()

    def last_chunk(j, _):
        edges(ITERS - 1, j)
        give(j).start()
        last_copy(j).start()

        @pl.when(j > 0)
        def _():
            fold(j - 1)

        return 0

    lax.fori_loop(0, CHUNKS, last_chunk, 0)
    fold(CHUNKS - 1)

    def toward(p, stage, by):
        return lax.rem(place[ORDERS[p][stage]] + by, 4)

    def block(p, stage, dest, half=None):
        index = [slice(None)] * 3
        for axis in ORDERS[p][:stage]:
            index[axis] = place[axis]
        index[ORDERS[p][stage]] = dest
        if half is not None:
            index[ORDERS[p][stage + 1]] = pl.ds(2 * half, 2)
        return (pl.ds(*PARTS[p]), *index)

    def message(p, kind):
        by = 1 if kind < 3 else 3
        return pltpu.make_async_remote_copy(
            src_ref=dense.at[block(p, 0, toward(p, 0, 2 if kind % 3 == 0 else by), 0 if kind in (0, 2, 4) else 1)],
            dst_ref=ring[p].at[kind],
            send_sem=post.at[p, kind],
            recv_sem=mail.at[p, kind],
            device_id=beside(ORDERS[p][0], by),
            device_id_type=MESH,
        )

    def straight(p, stage, by):
        return pltpu.make_async_remote_copy(
            src_ref=dense.at[block(p, stage, toward(p, stage, by))],
            dst_ref=(direct, final)[stage - 1][p].at[by - 1],
            send_sem=post.at[p, 3 + 3 * stage + by - 1],
            recv_sem=mail.at[p, 3 + 3 * stage + by - 1],
            device_id=beside(ORDERS[p][stage], by),
            device_id_type=MESH,
        )

    def add(where, *terms):
        total = dense[where]
        for term in terms:
            total = total + term
        dense[where] = total

    for p in range(3):
        message(p, 0).start()
        message(p, 3).start()
    for p in range(3):
        message(p, 1).start()
        message(p, 4).start()
    for p in range(3):
        message(p, 0).wait_recv()
        add(block(p, 0, toward(p, 0, 1), 0), ring[p][0])
        message(p, 2).start()
        message(p, 3).wait_recv()
        add(block(p, 0, toward(p, 0, 3), 1), ring[p][3])
        message(p, 5).start()
    for p in range(3):
        for kind in (1, 4, 2, 5):
            message(p, kind).wait_recv()
        add(block(p, 0, toward(p, 0, 0), 0), ring[p][2], ring[p][4])
        add(block(p, 0, toward(p, 0, 0), 1), ring[p][1], ring[p][5])
        for by in (2, 1, 3):
            straight(p, 1, by).start()
    for stage in (1, 2):
        for p in range(3):
            for by in (2, 1, 3):
                straight(p, stage, by).wait_recv()
            got = (direct, final)[stage - 1][p]
            add(block(p, stage, toward(p, stage, 0)), got[0], got[1], got[2])
            if stage == 1:
                for by in (2, 1, 3):
                    straight(p, 2, by).start()
    for tile in range(BY * CZ // LANES):
        out[0, :, tile * LANES : (tile + 1) * LANES] = dense[(tile, *place)]

    for p in range(3):
        for kind in range(6):
            message(p, kind).wait_send()
        for stage in (1, 2):
            for by in (1, 2, 3):
                straight(p, stage, by).wait_send()

    def finish(j, _):
        last_copy(j).wait()
        give(j).wait_send()
        rows = pl.ds(j * ROWS, ROWS)

        @pl.when(has_left)
        def _():
            to_left(0, j, now.at[0, pl.ds(0, 4), rows]).wait_send()

        @pl.when(has_right)
        def _():
            to_right(0, j, now.at[0, pl.ds(NX - 4, 4), rows]).wait_send()

        return 0

    lax.fori_loop(0, CHUNKS, finish, 0)
    key_swap.wait_send()
    prior_copy.wait()


def run(now, before, courant, source, tiles_here, slots_here):
    field = pltpu.VMEM((1, NX, CY, CZ), jnp.float32)
    ring, direct, final = [], [], []
    for order, (_, tiles) in zip(ORDERS, PARTS):
        sizes = [2 if axis == order[1] else 4 for axis in range(3) if axis != order[0]]
        ring.append(pltpu.VMEM((6, tiles, *sizes, TSLOTS, LANES), jnp.float32))
        direct.append(pltpu.VMEM((3, tiles, 4, TSLOTS, LANES), jnp.float32))
        final.append(pltpu.VMEM((3, tiles, TSLOTS, LANES), jnp.float32))
    halves = CZ // LANES
    return pl.pallas_call(
        kernel,
        out_shape=(field, field, pltpu.VMEM((1, TSLOTS, BY * CZ), jnp.float32)),
        in_specs=[pl.BlockSpec(memory_space=pl.ANY)] * 4 + [pl.BlockSpec(memory_space=pltpu.VMEM)] * 2,
        out_specs=(pl.BlockSpec(memory_space=pltpu.VMEM),) * 3,
        scratch_shapes=[
            pltpu.VMEM((2, NX + 8, CY + 2 * PAD, CZ), jnp.float32),
            pltpu.VMEM((NX, CY, CZ), jnp.float32),
            pltpu.VMEM((ITERS, NX, CY, CZ), jnp.bfloat16),
            pltpu.VMEM((CHUNKS, halves, NX * ROWS, LANES), jnp.float32),
            pltpu.VMEM((CHUNKS, halves, NX * ROWS, LANES), jnp.float32),
            pltpu.VMEM((GROUP, ROWS, CZ), jnp.float32),
            pltpu.VMEM((CZ, CZ), jnp.bfloat16),
            pltpu.VMEM((GROUP * ROWS, GROUP * WIDE), jnp.bfloat16),
            pltpu.VMEM((CHUNKS, LANES), jnp.float32),
            pltpu.VMEM((CHUNKS, LANES), jnp.float32),
            pltpu.VMEM((BY, 4 * STEP_BLOCKS, CZ), jnp.bfloat16),
            pltpu.VMEM((BY * halves, 4, 4, 4, TSLOTS, LANES), jnp.float32),
            *ring,
            *direct,
            *final,
            pltpu.SemaphoreType.DMA((3 + ITERS,)),
            pltpu.SemaphoreType.DMA((2, ITERS, CHUNKS)),
            pltpu.SemaphoreType.DMA((2, ITERS, CHUNKS)),
            pltpu.SemaphoreType.DMA((CHUNKS + 1,)),
            pltpu.SemaphoreType.DMA((2, CHUNKS + 1)),
            pltpu.SemaphoreType.DMA((3, 12)),
            pltpu.SemaphoreType.DMA((3, 12)),
        ],
        compiler_params=pltpu.CompilerParams(collective_id=0, has_side_effects=True, vmem_limit_bytes=59 * MIB),
        cost_estimate=pl.CostEstimate(flops=5_000_000_000, bytes_accessed=16_000_000, transcendentals=0),
    )(now, before, courant, source, tiles_here, slots_here)


def keep(*refs):
    semaphores = refs[6]
    copies = [pltpu.make_async_copy(refs[i], refs[3 + i], semaphores.at[i]) for i in range(3)]
    for copy in copies:
        copy.start()
    for copy in copies:
        copy.wait()


def on_device(wave_now, wave_before, courant, source_waves, tile_ids, slot_ids):
    results = run(wave_now, wave_before, courant, source_waves, tile_ids.reshape(1, NBLK), slot_ids.reshape(1, NBLK))
    return pl.pallas_call(
        keep,
        out_shape=tuple(jax.ShapeDtypeStruct(v.shape, v.dtype) for v in results),
        in_specs=[pl.BlockSpec(memory_space=pl.ANY)] * 3,
        out_specs=(pl.BlockSpec(memory_space=pl.ANY),) * 3,
        scratch_shapes=[pltpu.SemaphoreType.DMA((3,))],
        compiler_params=pltpu.CompilerParams(vmem_limit_bytes=MIB),
    )(*results)


def solution(mesh):
    return jax.shard_map(
        on_device,
        mesh=mesh,
        in_specs=(
            P("shot", "sub"),
            P("shot", "sub"),
            P("shot", "sub"),
            P(None, "shot", "sub"),
            P("shot", "sub", None),
            P("shot", "sub"),
        ),
        out_specs=(
            P("shot", "sub"),
            P("shot", "sub"),
            P(("shot", "sub")),
        ),
        check_vma=False,
    )
```

```python
import functools

import jax
import jax.numpy as jnp
from jax import lax
from jax.experimental import pallas as pl
from jax.experimental.pallas import tpu as pltpu
from jax.sharding import PartitionSpec as P

MESH = pl.DeviceIdType.MESH
MIB = 1024 * 1024
ITERS = 4
BY = 4
TSLOTS = 16
W = (-205.0 / 72.0, 8.0 / 5.0, -1.0 / 5.0, 8.0 / 315.0, -1.0 / 560.0)

NX, CY, CZ = 16, 128, 256
NBLK = NX * CY // BY
LANES = 128
HALVES = CZ // LANES
ROWS = 16
CHUNKS = CY // ROWS
PAD = 8
WIDE = ROWS + 2 * PAD
GROUP = 8
INNER, OUTER = 0, 1
LAYERS = ((4, 8), (0, 12))
XB = 2
HELD = GROUP * ROWS // BY
PAIR = 2 * HELD
FOLDS = CHUNKS // 2
PARTS = (
    (0, 2, (0, 1, 2)),
    (2, 2, (1, 0, 2)),
    (4, 1, (2, 0, 1)),
    (5, 1, (2, 1, 0)),
    (6, 1, (0, 1, 2)),
    (7, 1, (1, 0, 2)),
)
EARLY, LATE = (0, 1), (2, 3, 4, 5)


def bf(v):
    return v.astype(jnp.bfloat16)


def f32(v):
    return v.astype(jnp.float32)


def grid(shape, axis):
    return lax.broadcasted_iota(jnp.int32, shape, axis)


def kernel(now, before, courant, source, tiles_here, slots_here, last, prior, out, wave, speed, src, part, other, *rest):
    (zpart, zlast, band, across, keys, other_keys, rhs, dense), rest = rest[:8], rest[8:]
    count_parts = len(PARTS)
    ring, direct, final = (rest[i * count_parts : (i + 1) * count_parts] for i in range(3))
    load, send, recv, store, swap, key_sem, post, mail = rest[3 * count_parts :]
    shot = lax.axis_index("shot")
    sub = lax.axis_index("sub")
    count = lax.axis_size("sub")
    core = lax.rem(shot, 2)
    place = (shot // 2, sub // 4, lax.rem(sub, 4))
    has_left = sub > 0
    has_right = sub < count - 1
    left = (shot, jnp.maximum(sub - 1, 0))
    right = (shot, jnp.minimum(sub + 1, count - 1))
    partner = (shot + 1 - 2 * core, sub)

    def beside(axis, by):
        x, z, y = (lax.rem(c + by, 4) if a == axis else c for a, c in enumerate(place))
        return (x * 2 + core, z * 4 + y)

    barrier = pltpu.get_barrier_semaphore()

    @pl.when(has_left)
    def _():
        pl.semaphore_signal(barrier, inc=1, device_id=left, device_id_type=MESH)

    @pl.when(has_right)
    def _():
        pl.semaphore_signal(barrier, inc=1, device_id=right, device_id_type=MESH)

    for device in [partner] + [beside(axis, by) for axis in range(3) for by in (2, 1, 3)]:
        pl.semaphore_signal(barrier, inc=1, device_id=device, device_id_type=MESH)

    inner = (pl.ds(4, NX), pl.ds(PAD, CY))
    loads = [
        pltpu.make_async_copy(now.at[0], wave.at[(0, *inner)], load.at[0]),
        pltpu.make_async_copy(before.at[0], wave.at[(1, *inner)], load.at[1]),
        pltpu.make_async_copy(courant.at[0], speed, load.at[2]),
    ]
    loads += [pltpu.make_async_copy(source.at[t, 0], src.at[t], load.at[3 + t]) for t in range(ITERS)]
    for copy in loads:
        copy.start()

    edge = jnp.zeros((2, 4, CY, CZ), jnp.float32)

    @pl.when(jnp.logical_not(has_left))
    def _():
        wave[:, 0:4, PAD : PAD + CY, :] = edge

    @pl.when(jnp.logical_not(has_right))
    def _():
        wave[:, NX + 4 : NX + 8, PAD : PAD + CY, :] = edge

    strip = jnp.zeros((2, NX, PAD, CZ), jnp.float32)
    wave[:, 4 : NX + 4, 0:PAD, :] = strip
    wave[:, 4 : NX + 4, PAD + CY :, :] = strip

    def taps(gap):
        weights = jnp.zeros(gap.shape, jnp.float32)
        for k in range(1, 5):
            weights = jnp.where(gap == k, W[k] / W[1], weights)
        return weights

    band[...] = bf(taps(jnp.abs(grid((CZ, CZ), 0) - grid((CZ, CZ), 1))))
    shape = (GROUP * ROWS, GROUP * WIDE)
    gap = jnp.abs(lax.rem(grid(shape, 0), ROWS) + PAD - lax.rem(grid(shape, 1), WIDE))
    across[...] = bf(jnp.where(grid(shape, 0) // ROWS == grid(shape, 1) // WIDE, taps(gap), 0.0))

    pl.semaphore_wait(barrier, jnp.where(has_left, 1, 0) + jnp.where(has_right, 1, 0) + 10)

    def to_left(t, j, source_ref=None):
        b = lax.rem(t, 2)
        rows = pl.ds(PAD + j * ROWS, ROWS)
        return pltpu.make_async_remote_copy(
            src_ref=source_ref if source_ref is not None else wave.at[b, pl.ds(4, 4), rows],
            dst_ref=wave.at[b, pl.ds(NX + 4, 4), rows],
            send_sem=send.at[0, t, j],
            recv_sem=recv.at[0, t, j],
            device_id=left,
            device_id_type=MESH,
        )

    def to_right(t, j, source_ref=None):
        b = lax.rem(t, 2)
        rows = pl.ds(PAD + j * ROWS, ROWS)
        return pltpu.make_async_remote_copy(
            src_ref=source_ref if source_ref is not None else wave.at[b, pl.ds(NX, 4), rows],
            dst_ref=wave.at[b, pl.ds(0, 4), rows],
            send_sem=send.at[1, t, j],
            recv_sem=recv.at[1, t, j],
            device_id=right,
            device_id_type=MESH,
        )

    def first(j, _):
        rows = pl.ds(j * ROWS, ROWS)

        @pl.when(has_left)
        def _():
            to_left(0, j, now.at[0, pl.ds(0, 4), rows]).start()

        @pl.when(has_right)
        def _():
            to_right(0, j, now.at[0, pl.ds(NX - 4, 4), rows]).start()

        return 0

    lax.fori_loop(0, CHUNKS, first, 0)

    def keyed(b):
        x, j, g = b // (CY // BY), lax.rem(b // (ROWS // BY), CHUNKS), lax.rem(b, ROWS // BY)
        outer = jnp.logical_or(x < 4, x >= 12)
        place_in = jnp.where(outer, jnp.where(x < 4, x, x - 8), x - 4)
        return jnp.where(outer, FOLDS, 0) + j // 2, lax.rem(j, 2) * HELD + place_in * (ROWS // BY) + g

    spread = bf(f32(lax.rem(grid((NBLK, LANES), 1), PAIR) == keyed(grid((NBLK, LANES), 0))[1]))
    in_fold = keyed(grid((2 * FOLDS, NBLK), 1))[0] == grid((2 * FOLDS, NBLK), 0)
    named_tile, named_slot = (
        jnp.dot(bf(jnp.where(in_fold, f32(ref[...]), 0.0)), spread, preferred_element_type=jnp.float32)
        for ref in (tiles_here, slots_here)
    )
    keys[...] = named_tile * TSLOTS + named_slot
    key_swap = pltpu.make_async_remote_copy(
        src_ref=keys, dst_ref=other_keys, send_sem=key_sem.at[0], recv_sem=key_sem.at[1], device_id=partner, device_id_type=MESH
    )
    key_swap.start()
    dense[...] = jnp.zeros_like(dense)
    part[...] = jnp.zeros_like(part)

    for copy in loads[:4]:
        copy.wait()

    def mix(t, j, kind):
        cur = lax.rem(t, 2)
        window = pl.ds(pl.multiple_of(j * ROWS, ROWS), WIDE)
        v = jnp.concatenate([wave[cur, 4 + a : 8 + a, window, :] for a in LAYERS[kind]], axis=0).reshape(GROUP * WIDE, CZ)
        hi = bf(v)
        lo = bf(v - f32(hi))
        deep = jnp.dot(hi, band[...], preferred_element_type=jnp.float32)
        deep += jnp.dot(lo, band[...], preferred_element_type=jnp.float32)
        flat = jnp.dot(across[...], hi, preferred_element_type=jnp.float32)
        flat += jnp.dot(across[...], lo, preferred_element_type=jnp.float32)
        return deep.reshape(GROUP, WIDE, CZ)[:, PAD : PAD + ROWS] + flat.reshape(GROUP, ROWS, CZ)

    def update(t, j, kind, mixed, halves):
        cur = lax.rem(t, 2)
        nxt = 1 - cur
        rows = pl.ds(pl.multiple_of(PAD + j * ROWS, 8), ROWS)
        plain = pl.ds(pl.multiple_of(j * ROWS, ROWS), ROWS)
        deep = slice(halves[0] * LANES, (halves[-1] + 1) * LANES)
        block = 2 * XB // len(halves)
        for i in range(0, GROUP, block):
            x = LAYERS[kind][i // 4] + i % 4
            here = slice(x, x + block)
            center = wave[cur, x + 4 : x + 4 + block, rows, deep]
            lap = 3.0 * W[0] / W[1] * center + mixed[i : i + block, :, deep]
            for k in range(1, 5):
                pair = wave[cur, x + 4 + k : x + 4 + k + block, rows, deep] + wave[cur, x + 4 - k : x + 4 - k + block, rows, deep]
                lap += pair if k == 1 else W[k] / W[1] * pair
            after = 2.0 * center - wave[nxt, x + 4 : x + 4 + block, rows, deep] + W[1] * speed[here, plain, deep] * lap
            wave[nxt, x + 4 : x + 4 + block, rows, deep] = after
            term = (f32(src[t, here, plain, deep]) * after).reshape(block * ROWS, len(halves) * LANES)
            there = slice(i * ROWS, (i + block) * ROWS)
            for n, h in enumerate(halves):
                part[kind, j, h, there, :] += term[:, n * LANES : (n + 1) * LANES]

    def group(t, j, kind):
        zpart[...] = mix(t, j, kind)
        update(t, j, kind, zpart, (0, 1))

    def edges(t, j, send_on):
        @pl.when(has_left)
        def _():
            to_right(t, j).wait_recv()

            @pl.when(t > 0)
            def _():
                to_left(t, j).wait_send()

        @pl.when(has_right)
        def _():
            to_left(t, j).wait_recv()

            @pl.when(t > 0)
            def _():
                to_right(t, j).wait_send()

        group(t, j, OUTER)
        send_on(j)

    def send_whole(t, j):
        @pl.when(has_left)
        def _():
            to_left(t, j).start()

        @pl.when(has_right)
        def _():
            to_right(t, j).start()

    def half_to(side, h, j):
        b = (ITERS - 1) % 2
        rows = pl.ds(PAD + j * ROWS, ROWS)
        deep = pl.ds(h * LANES, LANES)
        here, there = ((4, NX + 4), (NX, 0))[side]
        return pltpu.make_async_remote_copy(
            src_ref=wave.at[b, pl.ds(here, 4), rows, deep],
            dst_ref=wave.at[b, pl.ds(there, 4), rows, deep],
            send_sem=send.at[side, ITERS - 1 + h, j],
            recv_sem=recv.at[side, ITERS - 1 + h, j],
            device_id=(left, right)[side],
            device_id_type=MESH,
        )

    def send_half(h, j):
        @pl.when(has_left)
        def _():
            half_to(0, h, j).start()

        @pl.when(has_right)
        def _():
            half_to(1, h, j).start()

    def last_edges(h, j):
        if h == 0:
            zlast[j] = mix(ITERS - 1, j, OUTER)

        @pl.when(has_left)
        def _():
            half_to(1, h, j).wait_recv()

        @pl.when(has_right)
        def _():
            half_to(0, h, j).wait_recv()

        update(ITERS - 1, j, OUTER, zlast.at[j], (h,))

    def last_copy(j):
        rows = pl.ds(pl.multiple_of(PAD + j * ROWS, 8), ROWS)
        plain = pl.ds(pl.multiple_of(j * ROWS, ROWS), ROWS)
        return pltpu.make_async_copy(wave.at[ITERS % 2, pl.ds(4, NX), rows], last.at[0, :, plain], store.at[j])

    prior_copy = pltpu.make_async_copy(wave.at[((ITERS + 1) % 2, *inner)], prior.at[0], store.at[CHUNKS])

    def give(j, half=None):
        index = (INNER, j) if half is None else (OUTER, j, half)
        which = 0 if half is None else 1 + half
        return pltpu.make_async_remote_copy(
            src_ref=part.at[index],
            dst_ref=other.at[index],
            send_sem=swap.at[0, which, j],
            recv_sem=swap.at[1, which, j],
            device_id=partner,
            device_id_type=MESH,
        )

    row_at = grid((1024, 1), 0)
    slot_row = f32(row_at // 256 * 512 + lax.rem(row_at, 256))
    lane = grid((1, LANES), 1)

    def fold(pair, half=None):
        kind, halves = (INNER, (0, 1)) if half is None else (OUTER, (half,))
        for j in (2 * pair, 2 * pair + 1):
            give(j, half).wait_recv()
        for h in halves:
            for r in range(BY):
                both = jnp.concatenate(
                    [ref[kind, 2 * pair + j, h, pl.ds(r, HELD, stride=BY), :] for ref in (part, other) for j in (0, 1)], axis=0
                )
                hi = bf(both)
                there = slice(r % 2 * LANES, (r % 2 + 1) * LANES)
                rhs[h, r // 2, 0:LANES, there] = hi
                rhs[h, r // 2, LANES : 2 * LANES, there] = bf(both - f32(hi))
        row = pl.ds(kind * FOLDS + pair, 1)
        named = jnp.where(lane < PAIR, keys[row, :], other_keys[row, :])
        named = jnp.concatenate([named, named], axis=1)

        def tiles(i, _):
            first = i * 4
            pick = bf(f32(named - f32(first * 512 + core * 256) == slot_row))
            for h in halves:
                for r in range(0, BY, 2):
                    sums = jnp.dot(pick, rhs[h, r // 2], preferred_element_type=jnp.float32)
                    for n in range(2):
                        dense[h * BY + r + n, pl.ds(first, 4)] += sums[:, n * LANES : (n + 1) * LANES].reshape(4, 4, 4, TSLOTS, LANES)
            return 0

        lax.fori_loop(0, 1, tiles, 0)

    def each(body):
        lax.fori_loop(0, CHUNKS, lambda j, _: (body(j), 0)[1], 0)

    each(lambda j: group(0, j, INNER))

    def one_step(t, _):
        for s in range(ITERS - 2):

            @pl.when(t == s)
            def _():
                loads[4 + s].wait()

        def one_chunk(j):
            edges(t, j, lambda j: send_whole(t + 1, j))

            @pl.when(j > 0)
            def _():
                group(t + 1, j - 1, INNER)

        each(one_chunk)
        group(t + 1, CHUNKS - 1, INNER)
        return 0

    lax.fori_loop(0, ITERS - 2, one_step, 0)
    loads[2 + ITERS].wait()
    key_swap.wait_recv()

    def third_chunk(j):
        edges(ITERS - 2, j, lambda j: send_half(0, j))

        @pl.when(j > 0)
        def _():
            group(ITERS - 1, j - 1, INNER)
            give(j - 1).start()

        @pl.when(jnp.logical_and(j >= 3, lax.rem(j, 2) == 1))
        def _():
            fold((j - 3) // 2)

    each(third_chunk)
    prior_copy.start()
    group(ITERS - 1, CHUNKS - 1, INNER)
    give(CHUNKS - 1).start()

    def last_chunk(h, j):
        if h == 0:
            send_half(1, j)
        last_edges(h, j)
        give(j, h).start()
        if h == 0:

            @pl.when(j == 1)
            def _():
                fold(FOLDS - 1)

        else:
            last_copy(j).start()

        @pl.when(jnp.logical_and(j >= 3, lax.rem(j, 2) == 1))
        def _():
            fold((j - 3) // 2, h)

    def toward(p, stage, by):
        return lax.rem(place[PARTS[p][2][stage]] + by, 4)

    def block(p, stage, dest, half=None):
        tile, tiles, order = PARTS[p]
        index = [slice(None)] * 3
        for axis in order[:stage]:
            index[axis] = place[axis]
        index[order[stage]] = dest
        if half is not None:
            index[order[stage + 1]] = pl.ds(2 * half, 2)
        return (pl.ds(tile, tiles), *index)

    def message(p, kind):
        by = 1 if kind < 3 else 3
        return pltpu.make_async_remote_copy(
            src_ref=dense.at[block(p, 0, toward(p, 0, 2 if kind % 3 == 0 else by), 0 if kind in (0, 2, 4) else 1)],
            dst_ref=ring[p].at[kind],
            send_sem=post.at[p, kind],
            recv_sem=mail.at[p, kind],
            device_id=beside(PARTS[p][2][0], by),
            device_id_type=MESH,
        )

    def straight(p, stage, by):
        return pltpu.make_async_remote_copy(
            src_ref=dense.at[block(p, stage, toward(p, stage, by))],
            dst_ref=(direct, final)[stage - 1][p].at[by - 1],
            send_sem=post.at[p, 3 + 3 * stage + by - 1],
            recv_sem=mail.at[p, 3 + 3 * stage + by - 1],
            device_id=beside(PARTS[p][2][stage], by),
            device_id_type=MESH,
        )

    def add(where, *terms):
        total = dense[where]
        for term in terms:
            total = total + term
        dense[where] = total

    def far(p):
        message(p, 0).start()
        message(p, 3).start()

    def near(p):
        message(p, 1).start()
        message(p, 4).start()

    def merged(p):
        message(p, 0).wait_recv()
        add(block(p, 0, toward(p, 0, 1), 0), ring[p][0])
        message(p, 2).start()
        message(p, 3).wait_recv()
        add(block(p, 0, toward(p, 0, 3), 1), ring[p][3])
        message(p, 5).start()

    def second(p):
        for kind in (1, 4, 2, 5):
            message(p, kind).wait_recv()
        add(block(p, 0, toward(p, 0, 0), 0), ring[p][2], ring[p][4])
        add(block(p, 0, toward(p, 0, 0), 1), ring[p][1], ring[p][5])
        for by in (2, 1, 3):
            straight(p, 1, by).start()

    def third(p):
        for by in (2, 1, 3):
            straight(p, 1, by).wait_recv()
        add(block(p, 1, toward(p, 1, 0)), direct[p][0], direct[p][1], direct[p][2])
        for by in (2, 1, 3):
            straight(p, 2, by).start()

    def done(p):
        for by in (2, 1, 3):
            straight(p, 2, by).wait_recv()
        tile, tiles, _ = PARTS[p]
        for i in range(tiles):
            total = dense[(tile + i, *place)] + final[p][0, i] + final[p][1, i] + final[p][2, i]
            first_lane = ((tile + i) % BY * HALVES + (tile + i) // BY) * LANES
            out[0, :, first_lane : first_lane + LANES] = total

    def carry_out(*plan):
        for action, parts in plan:
            for p in parts:
                action(p)

    each(functools.partial(last_chunk, 0))
    fold(FOLDS - 1, 0)
    carry_out((far, EARLY), (near, EARLY))
    each(functools.partial(last_chunk, 1))
    carry_out((merged, EARLY))
    fold(FOLDS - 1, 1)
    carry_out((far, LATE), (near, LATE), (second, EARLY), (merged, LATE), (second, LATE))
    carry_out((third, EARLY), (third, LATE), (done, EARLY), (done, LATE))

    for p in range(count_parts):
        for kind in range(6):
            message(p, kind).wait_send()
        for stage in (1, 2):
            for by in (1, 2, 3):
                straight(p, stage, by).wait_send()

    def finish(j):
        last_copy(j).wait()
        for half in (None, 0, 1):
            give(j, half).wait_send()
        rows = pl.ds(j * ROWS, ROWS)

        @pl.when(has_left)
        def _():
            to_left(0, j, now.at[0, pl.ds(0, 4), rows]).wait_send()
            for h in range(HALVES):
                half_to(0, h, j).wait_send()

        @pl.when(has_right)
        def _():
            to_right(0, j, now.at[0, pl.ds(NX - 4, 4), rows]).wait_send()
            for h in range(HALVES):
                half_to(1, h, j).wait_send()

    each(finish)
    key_swap.wait_send()
    prior_copy.wait()


def run(now, before, courant, source, tiles_here, slots_here):
    field = pltpu.VMEM((1, NX, CY, CZ), jnp.float32)
    ring, direct, final = [], [], []
    for _, tiles, order in PARTS:
        sizes = [2 if axis == order[1] else 4 for axis in range(3) if axis != order[0]]
        ring.append(pltpu.VMEM((6, tiles, *sizes, TSLOTS, LANES), jnp.float32))
        direct.append(pltpu.VMEM((3, tiles, 4, TSLOTS, LANES), jnp.float32))
        final.append(pltpu.VMEM((3, tiles, TSLOTS, LANES), jnp.float32))
    return pl.pallas_call(
        kernel,
        out_shape=(field, field, pltpu.VMEM((1, TSLOTS, BY * CZ), jnp.float32)),
        in_specs=[pl.BlockSpec(memory_space=pl.ANY)] * 4 + [pl.BlockSpec(memory_space=pltpu.VMEM)] * 2,
        out_specs=(pl.BlockSpec(memory_space=pltpu.VMEM),) * 3,
        scratch_shapes=[
            pltpu.VMEM((2, NX + 8, CY + 2 * PAD, CZ), jnp.float32),
            pltpu.VMEM((NX, CY, CZ), jnp.float32),
            pltpu.VMEM((ITERS, NX, CY, CZ), jnp.bfloat16),
            pltpu.VMEM((2, CHUNKS, HALVES, GROUP * ROWS, LANES), jnp.float32),
            pltpu.VMEM((2, CHUNKS, HALVES, GROUP * ROWS, LANES), jnp.float32),
            pltpu.VMEM((GROUP, ROWS, CZ), jnp.float32),
            pltpu.VMEM((CHUNKS, GROUP, ROWS, CZ), jnp.float32),
            pltpu.VMEM((CZ, CZ), jnp.bfloat16),
            pltpu.VMEM((GROUP * ROWS, GROUP * WIDE), jnp.bfloat16),
            pltpu.VMEM((2 * FOLDS, LANES), jnp.float32),
            pltpu.VMEM((2 * FOLDS, LANES), jnp.float32),
            pltpu.VMEM((HALVES, BY // 2, 4 * PAIR, 2 * LANES), jnp.bfloat16),
            pltpu.VMEM((BY * HALVES, 4, 4, 4, TSLOTS, LANES), jnp.float32),
            *ring,
            *direct,
            *final,
            pltpu.SemaphoreType.DMA((3 + ITERS,)),
            pltpu.SemaphoreType.DMA((2, ITERS + 1, CHUNKS)),
            pltpu.SemaphoreType.DMA((2, ITERS + 1, CHUNKS)),
            pltpu.SemaphoreType.DMA((CHUNKS + 1,)),
            pltpu.SemaphoreType.DMA((2, 3, CHUNKS)),
            pltpu.SemaphoreType.DMA((2,)),
            pltpu.SemaphoreType.DMA((len(PARTS), 12)),
            pltpu.SemaphoreType.DMA((len(PARTS), 12)),
        ],
        compiler_params=pltpu.CompilerParams(collective_id=0, has_side_effects=True, vmem_limit_bytes=59 * MIB),
        cost_estimate=pl.CostEstimate(flops=5_000_000_000, bytes_accessed=16_000_000, transcendentals=0),
    )(now, before, courant, source, tiles_here, slots_here)


def keep(*refs):
    semaphores = refs[6]
    copies = [pltpu.make_async_copy(refs[i], refs[3 + i], semaphores.at[i]) for i in range(3)]
    for copy in copies:
        copy.start()
    for copy in copies:
        copy.wait()


def on_device(wave_now, wave_before, courant, source_waves, tile_ids, slot_ids):
    results = run(wave_now, wave_before, courant, source_waves, tile_ids.reshape(1, NBLK), slot_ids.reshape(1, NBLK))
    return pl.pallas_call(
        keep,
        out_shape=tuple(jax.ShapeDtypeStruct(v.shape, v.dtype) for v in results),
        in_specs=[pl.BlockSpec(memory_space=pl.ANY)] * 3,
        out_specs=(pl.BlockSpec(memory_space=pl.ANY),) * 3,
        scratch_shapes=[pltpu.SemaphoreType.DMA((3,))],
        compiler_params=pltpu.CompilerParams(vmem_limit_bytes=MIB),
    )(*results)


def solution(mesh):
    return jax.shard_map(
        on_device,
        mesh=mesh,
        in_specs=(
            P("shot", "sub"),
            P("shot", "sub"),
            P("shot", "sub"),
            P(None, "shot", "sub"),
            P("shot", "sub", None),
            P("shot", "sub"),
        ),
        out_specs=(
            P("shot", "sub"),
            P("shot", "sub"),
            P(("shot", "sub")),
        ),
        check_vma=False,
    )
```

```python
import functools

import jax
import jax.numpy as jnp
from jax import lax
from jax.experimental import pallas as pl
from jax.experimental.pallas import tpu as pltpu
from jax.sharding import PartitionSpec as P

MESH = pl.DeviceIdType.MESH
MIB = 1024 * 1024
ITERS = 4
BY = 4
TSLOTS = 16
W = (-205.0 / 72.0, 8.0 / 5.0, -1.0 / 5.0, 8.0 / 315.0, -1.0 / 560.0)

NX, CY, CZ = 16, 128, 256
NBLK = NX * CY // BY
LANES = 128
HALVES = CZ // LANES
ROWS = 16
CHUNKS = CY // ROWS
PAD = 8
WIDE = ROWS + 2 * PAD
GROUP = 8
INNER, OUTER = 0, 1
LAYERS = ((4, 8), (0, 12))
XB = 2
HELD = GROUP * ROWS // BY
PAIR = 2 * HELD
FOLDS = CHUNKS // 2
PARTS = (
    (0, 2, (0, 1, 2)),
    (2, 2, (1, 0, 2)),
    (4, 1, (2, 0, 1)),
    (5, 1, (2, 1, 0)),
    (6, 1, (0, 1, 2)),
    (7, 1, (1, 0, 2)),
)
EARLY, LATE = (0, 1), (2, 3, 4, 5)
ALONG, OTHERS = (2, 3), (4, 5)


def bf(v):
    return v.astype(jnp.bfloat16)


def f32(v):
    return v.astype(jnp.float32)


def grid(shape, axis):
    return lax.broadcasted_iota(jnp.int32, shape, axis)


def kernel(now, before, courant, source, tiles_here, slots_here, last, prior, out, wave, speed, src, part, other, *rest):
    (zpart, zlast, band, across, keys, other_keys, rhs, dense), rest = rest[:8], rest[8:]
    count_parts = len(PARTS)
    ring, direct, final = (rest[i * count_parts : (i + 1) * count_parts] for i in range(3))
    load, send, recv, store, swap, key_sem, post, mail = rest[3 * count_parts :]
    shot = lax.axis_index("shot")
    sub = lax.axis_index("sub")
    count = lax.axis_size("sub")
    core = lax.rem(shot, 2)
    place = (shot // 2, sub // 4, lax.rem(sub, 4))
    has_left = sub > 0
    has_right = sub < count - 1
    left = (shot, jnp.maximum(sub - 1, 0))
    right = (shot, jnp.minimum(sub + 1, count - 1))
    partner = (shot + 1 - 2 * core, sub)

    def beside(axis, by):
        x, z, y = (lax.rem(c + by, 4) if a == axis else c for a, c in enumerate(place))
        return (x * 2 + core, z * 4 + y)

    barrier = pltpu.get_barrier_semaphore()

    @pl.when(has_left)
    def _():
        pl.semaphore_signal(barrier, inc=1, device_id=left, device_id_type=MESH)

    @pl.when(has_right)
    def _():
        pl.semaphore_signal(barrier, inc=1, device_id=right, device_id_type=MESH)

    for device in [partner] + [beside(axis, by) for axis in range(3) for by in (2, 1, 3)]:
        pl.semaphore_signal(barrier, inc=1, device_id=device, device_id_type=MESH)

    inner = (pl.ds(4, NX), pl.ds(PAD, CY))
    loads = [
        pltpu.make_async_copy(now.at[0], wave.at[(0, *inner)], load.at[0]),
        pltpu.make_async_copy(before.at[0], wave.at[(1, *inner)], load.at[1]),
        pltpu.make_async_copy(courant.at[0], speed, load.at[2]),
    ]
    loads += [pltpu.make_async_copy(source.at[t, 0], src.at[t], load.at[3 + t]) for t in range(ITERS)]
    for copy in loads:
        copy.start()

    edge = jnp.zeros((2, 4, CY, CZ), jnp.float32)

    @pl.when(jnp.logical_not(has_left))
    def _():
        wave[:, 0:4, PAD : PAD + CY, :] = edge

    @pl.when(jnp.logical_not(has_right))
    def _():
        wave[:, NX + 4 : NX + 8, PAD : PAD + CY, :] = edge

    strip = jnp.zeros((2, NX, PAD, CZ), jnp.float32)
    wave[:, 4 : NX + 4, 0:PAD, :] = strip
    wave[:, 4 : NX + 4, PAD + CY :, :] = strip

    def taps(gap):
        weights = jnp.zeros(gap.shape, jnp.float32)
        for k in range(1, 5):
            weights = jnp.where(gap == k, W[k] / W[1], weights)
        return weights

    band[...] = bf(taps(jnp.abs(grid((CZ, CZ), 0) - grid((CZ, CZ), 1))))
    shape = (GROUP * ROWS, GROUP * WIDE)
    gap = jnp.abs(lax.rem(grid(shape, 0), ROWS) + PAD - lax.rem(grid(shape, 1), WIDE))
    across[...] = bf(jnp.where(grid(shape, 0) // ROWS == grid(shape, 1) // WIDE, taps(gap), 0.0))

    pl.semaphore_wait(barrier, jnp.where(has_left, 1, 0) + jnp.where(has_right, 1, 0) + 10)

    def to_left(t, j, source_ref=None):
        b = lax.rem(t, 2)
        rows = pl.ds(PAD + j * ROWS, ROWS)
        return pltpu.make_async_remote_copy(
            src_ref=source_ref if source_ref is not None else wave.at[b, pl.ds(4, 4), rows],
            dst_ref=wave.at[b, pl.ds(NX + 4, 4), rows],
            send_sem=send.at[0, t, j],
            recv_sem=recv.at[0, t, j],
            device_id=left,
            device_id_type=MESH,
        )

    def to_right(t, j, source_ref=None):
        b = lax.rem(t, 2)
        rows = pl.ds(PAD + j * ROWS, ROWS)
        return pltpu.make_async_remote_copy(
            src_ref=source_ref if source_ref is not None else wave.at[b, pl.ds(NX, 4), rows],
            dst_ref=wave.at[b, pl.ds(0, 4), rows],
            send_sem=send.at[1, t, j],
            recv_sem=recv.at[1, t, j],
            device_id=right,
            device_id_type=MESH,
        )

    def first(j, _):
        rows = pl.ds(j * ROWS, ROWS)

        @pl.when(has_left)
        def _():
            to_left(0, j, now.at[0, pl.ds(0, 4), rows]).start()

        @pl.when(has_right)
        def _():
            to_right(0, j, now.at[0, pl.ds(NX - 4, 4), rows]).start()

        return 0

    lax.fori_loop(0, CHUNKS, first, 0)

    def keyed(b):
        x, j, g = b // (CY // BY), lax.rem(b // (ROWS // BY), CHUNKS), lax.rem(b, ROWS // BY)
        outer = jnp.logical_or(x < 4, x >= 12)
        place_in = jnp.where(outer, jnp.where(x < 4, x, x - 8), x - 4)
        return jnp.where(outer, FOLDS, 0) + j // 2, lax.rem(j, 2) * HELD + place_in * (ROWS // BY) + g

    spread = bf(f32(lax.rem(grid((NBLK, LANES), 1), PAIR) == keyed(grid((NBLK, LANES), 0))[1]))
    in_fold = keyed(grid((2 * FOLDS, NBLK), 1))[0] == grid((2 * FOLDS, NBLK), 0)
    named_tile, named_slot = (
        jnp.dot(bf(jnp.where(in_fold, f32(ref[...]), 0.0)), spread, preferred_element_type=jnp.float32)
        for ref in (tiles_here, slots_here)
    )
    keys[...] = named_tile * TSLOTS + named_slot
    key_swap = pltpu.make_async_remote_copy(
        src_ref=keys, dst_ref=other_keys, send_sem=key_sem.at[0], recv_sem=key_sem.at[1], device_id=partner, device_id_type=MESH
    )
    key_swap.start()
    dense[...] = jnp.zeros_like(dense)
    part[...] = jnp.zeros_like(part)

    for copy in loads[:4]:
        copy.wait()

    def mix(t, j, kind):
        cur = lax.rem(t, 2)
        window = pl.ds(pl.multiple_of(j * ROWS, ROWS), WIDE)
        v = jnp.concatenate([wave[cur, 4 + a : 8 + a, window, :] for a in LAYERS[kind]], axis=0).reshape(GROUP * WIDE, CZ)
        hi = bf(v)
        lo = bf(v - f32(hi))
        deep = jnp.dot(hi, band[...], preferred_element_type=jnp.float32)
        deep += jnp.dot(lo, band[...], preferred_element_type=jnp.float32)
        flat = jnp.dot(across[...], hi, preferred_element_type=jnp.float32)
        flat += jnp.dot(across[...], lo, preferred_element_type=jnp.float32)
        return deep.reshape(GROUP, WIDE, CZ)[:, PAD : PAD + ROWS] + flat.reshape(GROUP, ROWS, CZ)

    def update(t, j, kind, mixed, halves):
        cur = lax.rem(t, 2)
        nxt = 1 - cur
        rows = pl.ds(pl.multiple_of(PAD + j * ROWS, 8), ROWS)
        plain = pl.ds(pl.multiple_of(j * ROWS, ROWS), ROWS)
        deep = slice(halves[0] * LANES, (halves[-1] + 1) * LANES)
        block = 2 * XB // len(halves)
        for i in range(0, GROUP, block):
            x = LAYERS[kind][i // 4] + i % 4
            here = slice(x, x + block)
            center = wave[cur, x + 4 : x + 4 + block, rows, deep]
            lap = 3.0 * W[0] / W[1] * center + mixed[i : i + block, :, deep]
            for k in range(1, 5):
                pair = wave[cur, x + 4 + k : x + 4 + k + block, rows, deep] + wave[cur, x + 4 - k : x + 4 - k + block, rows, deep]
                lap += pair if k == 1 else W[k] / W[1] * pair
            after = 2.0 * center - wave[nxt, x + 4 : x + 4 + block, rows, deep] + W[1] * speed[here, plain, deep] * lap
            wave[nxt, x + 4 : x + 4 + block, rows, deep] = after
            term = (f32(src[t, here, plain, deep]) * after).reshape(block * ROWS, len(halves) * LANES)
            there = slice(i * ROWS, (i + block) * ROWS)
            for n, h in enumerate(halves):
                part[kind, j, h, there, :] += term[:, n * LANES : (n + 1) * LANES]

    def group(t, j, kind):
        zpart[...] = mix(t, j, kind)
        update(t, j, kind, zpart, (0, 1))

    def edges(t, j, send_on):
        @pl.when(has_left)
        def _():
            to_right(t, j).wait_recv()

            @pl.when(t > 0)
            def _():
                to_left(t, j).wait_send()

        @pl.when(has_right)
        def _():
            to_left(t, j).wait_recv()

            @pl.when(t > 0)
            def _():
                to_right(t, j).wait_send()

        group(t, j, OUTER)
        send_on(j)

    def send_whole(t, j):
        @pl.when(has_left)
        def _():
            to_left(t, j).start()

        @pl.when(has_right)
        def _():
            to_right(t, j).start()

    def half_to(side, h, j):
        b = (ITERS - 1) % 2
        rows = pl.ds(PAD + j * ROWS, ROWS)
        deep = pl.ds(h * LANES, LANES)
        here, there = ((4, NX + 4), (NX, 0))[side]
        return pltpu.make_async_remote_copy(
            src_ref=wave.at[b, pl.ds(here, 4), rows, deep],
            dst_ref=wave.at[b, pl.ds(there, 4), rows, deep],
            send_sem=send.at[side, ITERS - 1 + h, j],
            recv_sem=recv.at[side, ITERS - 1 + h, j],
            device_id=(left, right)[side],
            device_id_type=MESH,
        )

    def send_half(h, j):
        @pl.when(has_left)
        def _():
            half_to(0, h, j).start()

        @pl.when(has_right)
        def _():
            half_to(1, h, j).start()

    def last_edges(h, j):
        if h == 0:
            zlast[j] = mix(ITERS - 1, j, OUTER)

        @pl.when(has_left)
        def _():
            half_to(1, h, j).wait_recv()

        @pl.when(has_right)
        def _():
            half_to(0, h, j).wait_recv()

        update(ITERS - 1, j, OUTER, zlast.at[j], (h,))

    def last_copy(j):
        rows = pl.ds(pl.multiple_of(PAD + j * ROWS, 8), ROWS)
        plain = pl.ds(pl.multiple_of(j * ROWS, ROWS), ROWS)
        return pltpu.make_async_copy(wave.at[ITERS % 2, pl.ds(4, NX), rows], last.at[0, :, plain], store.at[j])

    prior_copy = pltpu.make_async_copy(wave.at[((ITERS + 1) % 2, *inner)], prior.at[0], store.at[CHUNKS])

    def give(j, half=None):
        index = (INNER, j) if half is None else (OUTER, j, half)
        which = 0 if half is None else 1 + half
        return pltpu.make_async_remote_copy(
            src_ref=part.at[index],
            dst_ref=other.at[index],
            send_sem=swap.at[0, which, j],
            recv_sem=swap.at[1, which, j],
            device_id=partner,
            device_id_type=MESH,
        )

    row_at = grid((1024, 1), 0)
    slot_row = f32(row_at // 256 * 512 + lax.rem(row_at, 256))
    lane = grid((1, LANES), 1)

    def fold(pair, half=None):
        kind, halves = (INNER, (0, 1)) if half is None else (OUTER, (half,))
        for j in (2 * pair, 2 * pair + 1):
            give(j, half).wait_recv()
        for h in halves:
            for r in range(BY):
                both = jnp.concatenate(
                    [ref[kind, 2 * pair + j, h, pl.ds(r, HELD, stride=BY), :] for ref in (part, other) for j in (0, 1)], axis=0
                )
                hi = bf(both)
                there = slice(r % 2 * LANES, (r % 2 + 1) * LANES)
                rhs[h, r // 2, 0:LANES, there] = hi
                rhs[h, r // 2, LANES : 2 * LANES, there] = bf(both - f32(hi))
        row = pl.ds(kind * FOLDS + pair, 1)
        named = jnp.where(lane < PAIR, keys[row, :], other_keys[row, :])
        named = jnp.concatenate([named, named], axis=1)

        def tiles(i, _):
            first = i * 4
            pick = bf(f32(named - f32(first * 512 + core * 256) == slot_row))
            for h in halves:
                for r in range(0, BY, 2):
                    sums = jnp.dot(pick, rhs[h, r // 2], preferred_element_type=jnp.float32)
                    for n in range(2):
                        dense[h * BY + r + n, pl.ds(first, 4)] += sums[:, n * LANES : (n + 1) * LANES].reshape(4, 4, 4, TSLOTS, LANES)
            return 0

        lax.fori_loop(0, 1, tiles, 0)

    def each(body, first=0, end=CHUNKS):
        lax.fori_loop(first, end, lambda j, _: (body(j), 0)[1], 0)

    each(lambda j: group(0, j, INNER))

    def one_step(t, _):
        for s in range(ITERS - 2):

            @pl.when(t == s)
            def _():
                loads[4 + s].wait()

        def one_chunk(j):
            edges(t, j, lambda j: send_whole(t + 1, j))

            @pl.when(j > 0)
            def _():
                group(t + 1, j - 1, INNER)

        each(one_chunk)
        group(t + 1, CHUNKS - 1, INNER)
        return 0

    lax.fori_loop(0, ITERS - 2, one_step, 0)
    loads[2 + ITERS].wait()
    key_swap.wait_recv()

    def third_chunk(j):
        edges(ITERS - 2, j, lambda j: send_half(0, j))

        @pl.when(j > 0)
        def _():
            group(ITERS - 1, j - 1, INNER)
            give(j - 1).start()

        @pl.when(jnp.logical_and(j >= 3, lax.rem(j, 2) == 1))
        def _():
            fold((j - 3) // 2)

    each(third_chunk)
    prior_copy.start()
    group(ITERS - 1, CHUNKS - 1, INNER)
    give(CHUNKS - 1).start()

    def last_chunk(h, j):
        if h == 0:
            send_half(1, j)
        last_edges(h, j)
        give(j, h).start()
        if h == 0:

            @pl.when(j == 1)
            def _():
                fold(FOLDS - 1)

        else:
            last_copy(j).start()

        @pl.when(jnp.logical_and(j >= 3, lax.rem(j, 2) == 1))
        def _():
            fold((j - 3) // 2, h)

    def toward(p, stage, by):
        return lax.rem(place[PARTS[p][2][stage]] + by, 4)

    def block(p, stage, dest, half=None):
        tile, tiles, order = PARTS[p]
        index = [slice(None)] * 3
        for axis in order[:stage]:
            index[axis] = place[axis]
        index[order[stage]] = dest
        if half is not None:
            index[order[stage + 1]] = pl.ds(2 * half, 2)
        return (pl.ds(tile, tiles), *index)

    def message(p, kind):
        by = 1 if kind < 3 else 3
        return pltpu.make_async_remote_copy(
            src_ref=dense.at[block(p, 0, toward(p, 0, 2 if kind % 3 == 0 else by), 0 if kind in (0, 2, 4) else 1)],
            dst_ref=ring[p].at[kind],
            send_sem=post.at[p, kind],
            recv_sem=mail.at[p, kind],
            device_id=beside(PARTS[p][2][0], by),
            device_id_type=MESH,
        )

    def straight(p, stage, by):
        return pltpu.make_async_remote_copy(
            src_ref=dense.at[block(p, stage, toward(p, stage, by))],
            dst_ref=(direct, final)[stage - 1][p].at[by - 1],
            send_sem=post.at[p, 3 + 3 * stage + by - 1],
            recv_sem=mail.at[p, 3 + 3 * stage + by - 1],
            device_id=beside(PARTS[p][2][stage], by),
            device_id_type=MESH,
        )

    def add(where, *terms):
        total = dense[where]
        for term in terms:
            total = total + term
        dense[where] = total

    def far(p):
        message(p, 0).start()
        message(p, 3).start()

    def near(p):
        message(p, 1).start()
        message(p, 4).start()

    def merged(p):
        message(p, 0).wait_recv()
        add(block(p, 0, toward(p, 0, 1), 0), ring[p][0])
        message(p, 2).start()
        message(p, 3).wait_recv()
        add(block(p, 0, toward(p, 0, 3), 1), ring[p][3])
        message(p, 5).start()

    def second(p):
        for kind in (1, 4, 2, 5):
            message(p, kind).wait_recv()
        add(block(p, 0, toward(p, 0, 0), 0), ring[p][2], ring[p][4])
        add(block(p, 0, toward(p, 0, 0), 1), ring[p][1], ring[p][5])
        for by in (2, 1, 3):
            straight(p, 1, by).start()

    def third(p):
        for by in (2, 1, 3):
            straight(p, 1, by).wait_recv()
        add(block(p, 1, toward(p, 1, 0)), direct[p][0], direct[p][1], direct[p][2])
        for by in (2, 1, 3):
            straight(p, 2, by).start()

    def done(p):
        for by in (2, 1, 3):
            straight(p, 2, by).wait_recv()
        tile, tiles, _ = PARTS[p]
        for i in range(tiles):
            total = dense[(tile + i, *place)] + final[p][0, i] + final[p][1, i] + final[p][2, i]
            first_lane = ((tile + i) % BY * HALVES + (tile + i) // BY) * LANES
            out[0, :, first_lane : first_lane + LANES] = total

    def carry_out(*plan):
        for action, parts in plan:
            for p in parts:
                action(p)

    each(functools.partial(last_chunk, 0))
    fold(FOLDS - 1, 0)
    carry_out((far, EARLY))
    each(functools.partial(last_chunk, 1), 0, 2)
    carry_out((near, EARLY))
    each(functools.partial(last_chunk, 1), 2, 8)
    carry_out((merged, EARLY))
    fold(FOLDS - 1, 1)
    carry_out((far, LATE))
    carry_out((near, LATE))
    carry_out((second, EARLY))
    carry_out((merged, LATE))
    carry_out((third, EARLY))
    carry_out((second, LATE))
    carry_out((done, EARLY))
    carry_out((third, LATE))
    carry_out((done, LATE))

    for p in range(count_parts):
        for kind in range(6):
            message(p, kind).wait_send()
        for stage in (1, 2):
            for by in (1, 2, 3):
                straight(p, stage, by).wait_send()

    def finish(j):
        last_copy(j).wait()
        for half in (None, 0, 1):
            give(j, half).wait_send()
        rows = pl.ds(j * ROWS, ROWS)

        @pl.when(has_left)
        def _():
            to_left(0, j, now.at[0, pl.ds(0, 4), rows]).wait_send()
            for h in range(HALVES):
                half_to(0, h, j).wait_send()

        @pl.when(has_right)
        def _():
            to_right(0, j, now.at[0, pl.ds(NX - 4, 4), rows]).wait_send()
            for h in range(HALVES):
                half_to(1, h, j).wait_send()

    each(finish)
    key_swap.wait_send()
    prior_copy.wait()


def run(now, before, courant, source, tiles_here, slots_here):
    field = pltpu.VMEM((1, NX, CY, CZ), jnp.float32)
    ring, direct, final = [], [], []
    for _, tiles, order in PARTS:
        sizes = [2 if axis == order[1] else 4 for axis in range(3) if axis != order[0]]
        ring.append(pltpu.VMEM((6, tiles, *sizes, TSLOTS, LANES), jnp.float32))
        direct.append(pltpu.VMEM((3, tiles, 4, TSLOTS, LANES), jnp.float32))
        final.append(pltpu.VMEM((3, tiles, TSLOTS, LANES), jnp.float32))
    return pl.pallas_call(
        kernel,
        out_shape=(field, field, pltpu.VMEM((1, TSLOTS, BY * CZ), jnp.float32)),
        in_specs=[pl.BlockSpec(memory_space=pl.ANY)] * 4 + [pl.BlockSpec(memory_space=pltpu.VMEM)] * 2,
        out_specs=(pl.BlockSpec(memory_space=pltpu.VMEM),) * 3,
        scratch_shapes=[
            pltpu.VMEM((2, NX + 8, CY + 2 * PAD, CZ), jnp.float32),
            pltpu.VMEM((NX, CY, CZ), jnp.float32),
            pltpu.VMEM((ITERS, NX, CY, CZ), jnp.bfloat16),
            pltpu.VMEM((2, CHUNKS, HALVES, GROUP * ROWS, LANES), jnp.float32),
            pltpu.VMEM((2, CHUNKS, HALVES, GROUP * ROWS, LANES), jnp.float32),
            pltpu.VMEM((GROUP, ROWS, CZ), jnp.float32),
            pltpu.VMEM((CHUNKS, GROUP, ROWS, CZ), jnp.float32),
            pltpu.VMEM((CZ, CZ), jnp.bfloat16),
            pltpu.VMEM((GROUP * ROWS, GROUP * WIDE), jnp.bfloat16),
            pltpu.VMEM((2 * FOLDS, LANES), jnp.float32),
            pltpu.VMEM((2 * FOLDS, LANES), jnp.float32),
            pltpu.VMEM((HALVES, BY // 2, 4 * PAIR, 2 * LANES), jnp.bfloat16),
            pltpu.VMEM((BY * HALVES, 4, 4, 4, TSLOTS, LANES), jnp.float32),
            *ring,
            *direct,
            *final,
            pltpu.SemaphoreType.DMA((3 + ITERS,)),
            pltpu.SemaphoreType.DMA((2, ITERS + 1, CHUNKS)),
            pltpu.SemaphoreType.DMA((2, ITERS + 1, CHUNKS)),
            pltpu.SemaphoreType.DMA((CHUNKS + 1,)),
            pltpu.SemaphoreType.DMA((2, 3, CHUNKS)),
            pltpu.SemaphoreType.DMA((2,)),
            pltpu.SemaphoreType.DMA((len(PARTS), 12)),
            pltpu.SemaphoreType.DMA((len(PARTS), 12)),
        ],
        compiler_params=pltpu.CompilerParams(collective_id=0, has_side_effects=True, vmem_limit_bytes=59 * MIB),
        cost_estimate=pl.CostEstimate(flops=5_000_000_000, bytes_accessed=16_000_000, transcendentals=0),
    )(now, before, courant, source, tiles_here, slots_here)


def keep(*refs):
    semaphores = refs[6]
    copies = [pltpu.make_async_copy(refs[i], refs[3 + i], semaphores.at[i]) for i in range(3)]
    for copy in copies:
        copy.start()
    for copy in copies:
        copy.wait()


def on_device(wave_now, wave_before, courant, source_waves, tile_ids, slot_ids):
    results = run(wave_now, wave_before, courant, source_waves, tile_ids.reshape(1, NBLK), slot_ids.reshape(1, NBLK))
    return pl.pallas_call(
        keep,
        out_shape=tuple(jax.ShapeDtypeStruct(v.shape, v.dtype) for v in results),
        in_specs=[pl.BlockSpec(memory_space=pl.ANY)] * 3,
        out_specs=(pl.BlockSpec(memory_space=pl.ANY),) * 3,
        scratch_shapes=[pltpu.SemaphoreType.DMA((3,))],
        compiler_params=pltpu.CompilerParams(vmem_limit_bytes=MIB),
    )(*results)


def solution(mesh):
    return jax.shard_map(
        on_device,
        mesh=mesh,
        in_specs=(
            P("shot", "sub"),
            P("shot", "sub"),
            P("shot", "sub"),
            P(None, "shot", "sub"),
            P("shot", "sub", None),
            P("shot", "sub"),
        ),
        out_specs=(
            P("shot", "sub"),
            P("shot", "sub"),
            P(("shot", "sub")),
        ),
        check_vma=False,
    )
```

```python
import functools

import jax
import jax.numpy as jnp
from jax import lax
from jax.experimental import pallas as pl
from jax.experimental.pallas import tpu as pltpu
from jax.sharding import PartitionSpec as P

MESH = pl.DeviceIdType.MESH
MIB = 1024 * 1024
ITERS = 4
BY = 4
TSLOTS = 16
W = (-205.0 / 72.0, 8.0 / 5.0, -1.0 / 5.0, 8.0 / 315.0, -1.0 / 560.0)

NX, CY, CZ = 16, 128, 256
NBLK = NX * CY // BY
LANES = 128
HALVES = CZ // LANES
ROWS = 16
CHUNKS = CY // ROWS
PAD = 8
WIDE = ROWS + 2 * PAD
GROUP = 8
INNER, OUTER = 0, 1
LAYERS = ((4, 8), (0, 12))
XB = 2
HELD = GROUP * ROWS // BY
PAIR = 2 * HELD
FOLDS = CHUNKS // 2
PARTS = (
    (0, 2, (0, 1, 2)),
    (2, 2, (1, 0, 2)),
    (4, 1, (2, 0, 1)),
    (5, 1, (2, 1, 0)),
    (6, 1, (0, 1, 2)),
    (7, 1, (1, 0, 2)),
)
EARLY, LATE = (0, 1), (2, 3, 4, 5)
ALONG, OTHERS = (2, 3), (4, 5)


def bf(v):
    return v.astype(jnp.bfloat16)


def f32(v):
    return v.astype(jnp.float32)


def grid(shape, axis):
    return lax.broadcasted_iota(jnp.int32, shape, axis)


def kernel(now, before, courant, source, tiles_here, slots_here, last, prior, out, wave, speed, src, part, other, *rest):
    (zpart, zlast, band, across, keys, other_keys, rhs, dense), rest = rest[:8], rest[8:]
    count_parts = len(PARTS)
    ring, direct, final = (rest[i * count_parts : (i + 1) * count_parts] for i in range(3))
    load, send, recv, store, swap, key_sem, post, mail = rest[3 * count_parts :]
    shot = lax.axis_index("shot")
    sub = lax.axis_index("sub")
    count = lax.axis_size("sub")
    core = lax.rem(shot, 2)
    place = (shot // 2, sub // 4, lax.rem(sub, 4))
    has_left = sub > 0
    has_right = sub < count - 1
    left = (shot, jnp.maximum(sub - 1, 0))
    right = (shot, jnp.minimum(sub + 1, count - 1))
    partner = (shot + 1 - 2 * core, sub)

    def beside(axis, by):
        x, z, y = (lax.rem(c + by, 4) if a == axis else c for a, c in enumerate(place))
        return (x * 2 + core, z * 4 + y)

    barrier = pltpu.get_barrier_semaphore()

    @pl.when(has_left)
    def _():
        pl.semaphore_signal(barrier, inc=1, device_id=left, device_id_type=MESH)

    @pl.when(has_right)
    def _():
        pl.semaphore_signal(barrier, inc=1, device_id=right, device_id_type=MESH)

    for device in [partner] + [beside(axis, by) for axis in range(3) for by in (2, 1, 3)]:
        pl.semaphore_signal(barrier, inc=1, device_id=device, device_id_type=MESH)

    inner = (pl.ds(4, NX), pl.ds(PAD, CY))
    loads = [
        pltpu.make_async_copy(now.at[0], wave.at[(0, *inner)], load.at[0]),
        pltpu.make_async_copy(before.at[0], wave.at[(1, *inner)], load.at[1]),
        pltpu.make_async_copy(courant.at[0], speed, load.at[2]),
    ]
    loads += [pltpu.make_async_copy(source.at[t, 0], src.at[t], load.at[3 + t]) for t in range(ITERS)]
    for copy in loads:
        copy.start()

    edge = jnp.zeros((2, 4, CY, CZ), jnp.float32)

    @pl.when(jnp.logical_not(has_left))
    def _():
        wave[:, 0:4, PAD : PAD + CY, :] = edge

    @pl.when(jnp.logical_not(has_right))
    def _():
        wave[:, NX + 4 : NX + 8, PAD : PAD + CY, :] = edge

    strip = jnp.zeros((2, NX, PAD, CZ), jnp.float32)
    wave[:, 4 : NX + 4, 0:PAD, :] = strip
    wave[:, 4 : NX + 4, PAD + CY :, :] = strip

    def taps(gap):
        weights = jnp.zeros(gap.shape, jnp.float32)
        for k in range(1, 5):
            weights = jnp.where(gap == k, W[k] / W[1], weights)
        return weights

    band[...] = bf(taps(jnp.abs(grid((CZ, CZ), 0) - grid((CZ, CZ), 1))))
    shape = (GROUP * ROWS, GROUP * WIDE)
    gap = jnp.abs(lax.rem(grid(shape, 0), ROWS) + PAD - lax.rem(grid(shape, 1), WIDE))
    across[...] = bf(jnp.where(grid(shape, 0) // ROWS == grid(shape, 1) // WIDE, taps(gap), 0.0))

    pl.semaphore_wait(barrier, jnp.where(has_left, 1, 0) + jnp.where(has_right, 1, 0) + 10)

    def to_left(t, j, source_ref=None):
        b = lax.rem(t, 2)
        rows = pl.ds(PAD + j * ROWS, ROWS)
        return pltpu.make_async_remote_copy(
            src_ref=source_ref if source_ref is not None else wave.at[b, pl.ds(4, 4), rows],
            dst_ref=wave.at[b, pl.ds(NX + 4, 4), rows],
            send_sem=send.at[0, t, j],
            recv_sem=recv.at[0, t, j],
            device_id=left,
            device_id_type=MESH,
        )

    def to_right(t, j, source_ref=None):
        b = lax.rem(t, 2)
        rows = pl.ds(PAD + j * ROWS, ROWS)
        return pltpu.make_async_remote_copy(
            src_ref=source_ref if source_ref is not None else wave.at[b, pl.ds(NX, 4), rows],
            dst_ref=wave.at[b, pl.ds(0, 4), rows],
            send_sem=send.at[1, t, j],
            recv_sem=recv.at[1, t, j],
            device_id=right,
            device_id_type=MESH,
        )

    def first(j, _):
        rows = pl.ds(j * ROWS, ROWS)

        @pl.when(has_left)
        def _():
            to_left(0, j, now.at[0, pl.ds(0, 4), rows]).start()

        @pl.when(has_right)
        def _():
            to_right(0, j, now.at[0, pl.ds(NX - 4, 4), rows]).start()

        return 0

    lax.fori_loop(0, CHUNKS, first, 0)

    def keyed(b):
        x, j, g = b // (CY // BY), lax.rem(b // (ROWS // BY), CHUNKS), lax.rem(b, ROWS // BY)
        outer = jnp.logical_or(x < 4, x >= 12)
        place_in = jnp.where(outer, jnp.where(x < 4, x, x - 8), x - 4)
        return jnp.where(outer, FOLDS, 0) + j // 2, lax.rem(j, 2) * HELD + place_in * (ROWS // BY) + g

    spread = bf(f32(lax.rem(grid((NBLK, LANES), 1), PAIR) == keyed(grid((NBLK, LANES), 0))[1]))
    in_fold = keyed(grid((2 * FOLDS, NBLK), 1))[0] == grid((2 * FOLDS, NBLK), 0)
    named_tile, named_slot = (
        jnp.dot(bf(jnp.where(in_fold, f32(ref[...]), 0.0)), spread, preferred_element_type=jnp.float32)
        for ref in (tiles_here, slots_here)
    )
    keys[...] = named_tile * TSLOTS + named_slot
    key_swap = pltpu.make_async_remote_copy(
        src_ref=keys, dst_ref=other_keys, send_sem=key_sem.at[0], recv_sem=key_sem.at[1], device_id=partner, device_id_type=MESH
    )
    key_swap.start()
    dense[...] = jnp.zeros_like(dense)
    part[...] = jnp.zeros_like(part)

    for copy in loads[:4]:
        copy.wait()

    def mix(t, j, kind):
        cur = lax.rem(t, 2)
        window = pl.ds(pl.multiple_of(j * ROWS, ROWS), WIDE)
        v = jnp.concatenate([wave[cur, 4 + a : 8 + a, window, :] for a in LAYERS[kind]], axis=0).reshape(GROUP * WIDE, CZ)
        hi = bf(v)
        lo = bf(v - f32(hi))
        deep = jnp.dot(hi, band[...], preferred_element_type=jnp.float32)
        deep += jnp.dot(lo, band[...], preferred_element_type=jnp.float32)
        flat = jnp.dot(across[...], hi, preferred_element_type=jnp.float32)
        flat += jnp.dot(across[...], lo, preferred_element_type=jnp.float32)
        return deep.reshape(GROUP, WIDE, CZ)[:, PAD : PAD + ROWS] + flat.reshape(GROUP, ROWS, CZ)

    def update(t, j, kind, mixed, halves):
        cur = lax.rem(t, 2)
        nxt = 1 - cur
        rows = pl.ds(pl.multiple_of(PAD + j * ROWS, 8), ROWS)
        plain = pl.ds(pl.multiple_of(j * ROWS, ROWS), ROWS)
        deep = slice(halves[0] * LANES, (halves[-1] + 1) * LANES)
        block = 2 * XB // len(halves)
        for i in range(0, GROUP, block):
            x = LAYERS[kind][i // 4] + i % 4
            here = slice(x, x + block)
            center = wave[cur, x + 4 : x + 4 + block, rows, deep]
            lap = 3.0 * W[0] / W[1] * center + mixed[i : i + block, :, deep]
            for k in range(1, 5):
                pair = wave[cur, x + 4 + k : x + 4 + k + block, rows, deep] + wave[cur, x + 4 - k : x + 4 - k + block, rows, deep]
                lap += pair if k == 1 else W[k] / W[1] * pair
            after = 2.0 * center - wave[nxt, x + 4 : x + 4 + block, rows, deep] + W[1] * speed[here, plain, deep] * lap
            wave[nxt, x + 4 : x + 4 + block, rows, deep] = after
            term = (f32(src[t, here, plain, deep]) * after).reshape(block * ROWS, len(halves) * LANES)
            there = slice(i * ROWS, (i + block) * ROWS)
            for n, h in enumerate(halves):
                part[kind, j, h, there, :] += term[:, n * LANES : (n + 1) * LANES]

    def group(t, j, kind):
        zpart[...] = mix(t, j, kind)
        update(t, j, kind, zpart, (0, 1))

    def edges(t, j, send_on):
        @pl.when(has_left)
        def _():
            to_right(t, j).wait_recv()

            @pl.when(t > 0)
            def _():
                to_left(t, j).wait_send()

        @pl.when(has_right)
        def _():
            to_left(t, j).wait_recv()

            @pl.when(t > 0)
            def _():
                to_right(t, j).wait_send()

        group(t, j, OUTER)
        send_on(j)

    def send_whole(t, j):
        @pl.when(has_left)
        def _():
            to_left(t, j).start()

        @pl.when(has_right)
        def _():
            to_right(t, j).start()

    def half_to(side, h, j):
        b = (ITERS - 1) % 2
        rows = pl.ds(PAD + j * ROWS, ROWS)
        deep = pl.ds(h * LANES, LANES)
        here, there = ((4, NX + 4), (NX, 0))[side]
        return pltpu.make_async_remote_copy(
            src_ref=wave.at[b, pl.ds(here, 4), rows, deep],
            dst_ref=wave.at[b, pl.ds(there, 4), rows, deep],
            send_sem=send.at[side, ITERS - 1 + h, j],
            recv_sem=recv.at[side, ITERS - 1 + h, j],
            device_id=(left, right)[side],
            device_id_type=MESH,
        )

    def send_half(h, j):
        @pl.when(has_left)
        def _():
            half_to(0, h, j).start()

        @pl.when(has_right)
        def _():
            half_to(1, h, j).start()

    def last_edges(h, j):
        if h == 0:
            zlast[j] = mix(ITERS - 1, j, OUTER)

        @pl.when(has_left)
        def _():
            half_to(1, h, j).wait_recv()

        @pl.when(has_right)
        def _():
            half_to(0, h, j).wait_recv()

        update(ITERS - 1, j, OUTER, zlast.at[j], (h,))

    def last_copy(j):
        rows = pl.ds(pl.multiple_of(PAD + j * ROWS, 8), ROWS)
        plain = pl.ds(pl.multiple_of(j * ROWS, ROWS), ROWS)
        return pltpu.make_async_copy(wave.at[ITERS % 2, pl.ds(4, NX), rows], last.at[0, :, plain], store.at[j])

    prior_copy = pltpu.make_async_copy(wave.at[((ITERS + 1) % 2, *inner)], prior.at[0], store.at[CHUNKS])

    def give(j, half=None):
        index = (INNER, j) if half is None else (OUTER, j, half)
        which = 0 if half is None else 1 + half
        return pltpu.make_async_remote_copy(
            src_ref=part.at[index],
            dst_ref=other.at[index],
            send_sem=swap.at[0, which, j],
            recv_sem=swap.at[1, which, j],
            device_id=partner,
            device_id_type=MESH,
        )

    row_at = grid((1024, 1), 0)
    slot_row = f32(row_at // 256 * 512 + lax.rem(row_at, 256))
    lane = grid((1, LANES), 1)

    def fold(pair, half=None):
        kind, halves = (INNER, (0, 1)) if half is None else (OUTER, (half,))
        for j in (2 * pair, 2 * pair + 1):
            give(j, half).wait_recv()
        for h in halves:
            for r in range(BY):
                both = jnp.concatenate(
                    [ref[kind, 2 * pair + j, h, pl.ds(r, HELD, stride=BY), :] for ref in (part, other) for j in (0, 1)], axis=0
                )
                hi = bf(both)
                there = slice(r % 2 * LANES, (r % 2 + 1) * LANES)
                rhs[h, r // 2, 0:LANES, there] = hi
                rhs[h, r // 2, LANES : 2 * LANES, there] = bf(both - f32(hi))
        row = pl.ds(kind * FOLDS + pair, 1)
        named = jnp.where(lane < PAIR, keys[row, :], other_keys[row, :])
        named = jnp.concatenate([named, named], axis=1)

        def tiles(i, _):
            first = i * 4
            pick = bf(f32(named - f32(first * 512 + core * 256) == slot_row))
            for h in halves:
                for r in range(0, BY, 2):
                    sums = jnp.dot(pick, rhs[h, r // 2], preferred_element_type=jnp.float32)
                    for n in range(2):
                        dense[h * BY + r + n, pl.ds(first, 4)] += sums[:, n * LANES : (n + 1) * LANES].reshape(4, 4, 4, TSLOTS, LANES)
            return 0

        lax.fori_loop(0, 1, tiles, 0)

    def each(body, first=0, end=CHUNKS):
        lax.fori_loop(first, end, lambda j, _: (body(j), 0)[1], 0)

    each(lambda j: group(0, j, INNER))

    def one_step(t, _):
        for s in range(ITERS - 2):

            @pl.when(t == s)
            def _():
                loads[4 + s].wait()

        def one_chunk(j):
            edges(t, j, lambda j: send_whole(t + 1, j))

            @pl.when(j > 0)
            def _():
                group(t + 1, j - 1, INNER)

        each(one_chunk)
        group(t + 1, CHUNKS - 1, INNER)
        return 0

    lax.fori_loop(0, ITERS - 2, one_step, 0)
    loads[2 + ITERS].wait()
    key_swap.wait_recv()

    def third_chunk(j):
        edges(ITERS - 2, j, lambda j: send_half(0, j))

        @pl.when(j > 0)
        def _():
            group(ITERS - 1, j - 1, INNER)
            give(j - 1).start()

        @pl.when(jnp.logical_and(j >= 3, lax.rem(j, 2) == 1))
        def _():
            fold((j - 3) // 2)

    each(third_chunk)
    prior_copy.start()
    group(ITERS - 1, CHUNKS - 1, INNER)
    give(CHUNKS - 1).start()

    def last_chunk(h, j):
        if h == 0:
            send_half(1, j)
        last_edges(h, j)
        give(j, h).start()
        if h == 0:

            @pl.when(j == 1)
            def _():
                fold(FOLDS - 1)

        else:
            last_copy(j).start()

        @pl.when(jnp.logical_and(j >= 3, lax.rem(j, 2) == 1))
        def _():
            fold((j - 3) // 2, h)

    def toward(p, stage, by):
        return lax.rem(place[PARTS[p][2][stage]] + by, 4)

    def block(p, stage, dest, half=None):
        tile, tiles, order = PARTS[p]
        index = [slice(None)] * 3
        for axis in order[:stage]:
            index[axis] = place[axis]
        index[order[stage]] = dest
        if half is not None:
            index[order[stage + 1]] = pl.ds(2 * half, 2)
        return (pl.ds(tile, tiles), *index)

    def message(p, kind):
        by = 1 if kind < 3 else 3
        return pltpu.make_async_remote_copy(
            src_ref=dense.at[block(p, 0, toward(p, 0, 2 if kind % 3 == 0 else by), 0 if kind in (0, 2, 4) else 1)],
            dst_ref=ring[p].at[kind],
            send_sem=post.at[p, kind],
            recv_sem=mail.at[p, kind],
            device_id=beside(PARTS[p][2][0], by),
            device_id_type=MESH,
        )

    def straight(p, stage, by):
        return pltpu.make_async_remote_copy(
            src_ref=dense.at[block(p, stage, toward(p, stage, by))],
            dst_ref=(direct, final)[stage - 1][p].at[by - 1],
            send_sem=post.at[p, 3 + 3 * stage + by - 1],
            recv_sem=mail.at[p, 3 + 3 * stage + by - 1],
            device_id=beside(PARTS[p][2][stage], by),
            device_id_type=MESH,
        )

    def add(where, *terms):
        total = dense[where]
        for term in terms:
            total = total + term
        dense[where] = total

    def far(p):
        message(p, 0).start()
        message(p, 3).start()

    def near(p):
        message(p, 1).start()
        message(p, 4).start()

    def merged(p):
        message(p, 0).wait_recv()
        add(block(p, 0, toward(p, 0, 1), 0), ring[p][0])
        message(p, 2).start()
        message(p, 3).wait_recv()
        add(block(p, 0, toward(p, 0, 3), 1), ring[p][3])
        message(p, 5).start()

    def second(p):
        for kind in (1, 4, 2, 5):
            message(p, kind).wait_recv()
        add(block(p, 0, toward(p, 0, 0), 0), ring[p][2], ring[p][4])
        add(block(p, 0, toward(p, 0, 0), 1), ring[p][1], ring[p][5])
        for by in (2, 1, 3):
            straight(p, 1, by).start()

    def third(p):
        for by in (2, 1, 3):
            straight(p, 1, by).wait_recv()
        add(block(p, 1, toward(p, 1, 0)), direct[p][0], direct[p][1], direct[p][2])
        for by in (2, 1, 3):
            straight(p, 2, by).start()

    def done(p):
        for by in (2, 1, 3):
            straight(p, 2, by).wait_recv()
        tile, tiles, _ = PARTS[p]
        for i in range(tiles):
            total = dense[(tile + i, *place)] + final[p][0, i] + final[p][1, i] + final[p][2, i]
            first_lane = ((tile + i) % BY * HALVES + (tile + i) // BY) * LANES
            out[0, :, first_lane : first_lane + LANES] = total

    def carry_out(*plan):
        for action, parts in plan:
            for p in parts:
                action(p)

    each(functools.partial(last_chunk, 0))
    fold(FOLDS - 1, 0)
    def sent(p, stage):
        for by in (1, 2, 3):
            straight(p, stage, by).wait_send()

    def sent_ring(p):
        for kind in range(6):
            message(p, kind).wait_send()
        sent(p, 1)

    def finish(j):
        last_copy(j).wait()
        for half in (None, 0, 1):
            give(j, half).wait_send()
        rows = pl.ds(j * ROWS, ROWS)

        @pl.when(has_left)
        def _():
            to_left(0, j, now.at[0, pl.ds(0, 4), rows]).wait_send()
            for h in range(HALVES):
                half_to(0, h, j).wait_send()

        @pl.when(has_right)
        def _():
            to_right(0, j, now.at[0, pl.ds(NX - 4, 4), rows]).wait_send()
            for h in range(HALVES):
                half_to(1, h, j).wait_send()

    carry_out((far, EARLY))
    each(functools.partial(last_chunk, 1), 0, 2)
    carry_out((near, EARLY))
    each(functools.partial(last_chunk, 1), 2, 8)
    carry_out((merged, EARLY))
    fold(FOLDS - 1, 1)
    carry_out((far, LATE))
    carry_out((near, LATE))
    each(finish)
    key_swap.wait_send()
    prior_copy.wait()
    carry_out((second, EARLY))
    carry_out((merged, LATE))
    carry_out((third, EARLY))
    carry_out((second, LATE))
    carry_out((sent_ring, EARLY))
    carry_out((done, EARLY))
    carry_out((third, LATE))
    carry_out((sent_ring, LATE))
    carry_out((done, LATE))

    for p in range(count_parts):
        sent(p, 2)


def run(now, before, courant, source, tiles_here, slots_here):
    field = pltpu.VMEM((1, NX, CY, CZ), jnp.float32)
    ring, direct, final = [], [], []
    for _, tiles, order in PARTS:
        sizes = [2 if axis == order[1] else 4 for axis in range(3) if axis != order[0]]
        ring.append(pltpu.VMEM((6, tiles, *sizes, TSLOTS, LANES), jnp.float32))
        direct.append(pltpu.VMEM((3, tiles, 4, TSLOTS, LANES), jnp.float32))
        final.append(pltpu.VMEM((3, tiles, TSLOTS, LANES), jnp.float32))
    return pl.pallas_call(
        kernel,
        out_shape=(field, field, pltpu.VMEM((1, TSLOTS, BY * CZ), jnp.float32)),
        in_specs=[pl.BlockSpec(memory_space=pl.ANY)] * 4 + [pl.BlockSpec(memory_space=pltpu.VMEM)] * 2,
        out_specs=(pl.BlockSpec(memory_space=pltpu.VMEM),) * 3,
        scratch_shapes=[
            pltpu.VMEM((2, NX + 8, CY + 2 * PAD, CZ), jnp.float32),
            pltpu.VMEM((NX, CY, CZ), jnp.float32),
            pltpu.VMEM((ITERS, NX, CY, CZ), jnp.bfloat16),
            pltpu.VMEM((2, CHUNKS, HALVES, GROUP * ROWS, LANES), jnp.float32),
            pltpu.VMEM((2, CHUNKS, HALVES, GROUP * ROWS, LANES), jnp.float32),
            pltpu.VMEM((GROUP, ROWS, CZ), jnp.float32),
            pltpu.VMEM((CHUNKS, GROUP, ROWS, CZ), jnp.float32),
            pltpu.VMEM((CZ, CZ), jnp.bfloat16),
            pltpu.VMEM((GROUP * ROWS, GROUP * WIDE), jnp.bfloat16),
            pltpu.VMEM((2 * FOLDS, LANES), jnp.float32),
            pltpu.VMEM((2 * FOLDS, LANES), jnp.float32),
            pltpu.VMEM((HALVES, BY // 2, 4 * PAIR, 2 * LANES), jnp.bfloat16),
            pltpu.VMEM((BY * HALVES, 4, 4, 4, TSLOTS, LANES), jnp.float32),
            *ring,
            *direct,
            *final,
            pltpu.SemaphoreType.DMA((3 + ITERS,)),
            pltpu.SemaphoreType.DMA((2, ITERS + 1, CHUNKS)),
            pltpu.SemaphoreType.DMA((2, ITERS + 1, CHUNKS)),
            pltpu.SemaphoreType.DMA((CHUNKS + 1,)),
            pltpu.SemaphoreType.DMA((2, 3, CHUNKS)),
            pltpu.SemaphoreType.DMA((2,)),
            pltpu.SemaphoreType.DMA((len(PARTS), 12)),
            pltpu.SemaphoreType.DMA((len(PARTS), 12)),
        ],
        compiler_params=pltpu.CompilerParams(collective_id=0, has_side_effects=True, vmem_limit_bytes=59 * MIB),
        cost_estimate=pl.CostEstimate(flops=5_000_000_000, bytes_accessed=16_000_000, transcendentals=0),
    )(now, before, courant, source, tiles_here, slots_here)


def keep(*refs):
    semaphores = refs[6]
    copies = [pltpu.make_async_copy(refs[i], refs[3 + i], semaphores.at[i]) for i in range(3)]
    for copy in copies:
        copy.start()
    for copy in copies:
        copy.wait()


def on_device(wave_now, wave_before, courant, source_waves, tile_ids, slot_ids):
    results = run(wave_now, wave_before, courant, source_waves, tile_ids.reshape(1, NBLK), slot_ids.reshape(1, NBLK))
    return pl.pallas_call(
        keep,
        out_shape=tuple(jax.ShapeDtypeStruct(v.shape, v.dtype) for v in results),
        in_specs=[pl.BlockSpec(memory_space=pl.ANY)] * 3,
        out_specs=(pl.BlockSpec(memory_space=pl.ANY),) * 3,
        scratch_shapes=[pltpu.SemaphoreType.DMA((3,))],
        compiler_params=pltpu.CompilerParams(vmem_limit_bytes=MIB),
    )(*results)


def solution(mesh):
    return jax.shard_map(
        on_device,
        mesh=mesh,
        in_specs=(
            P("shot", "sub"),
            P("shot", "sub"),
            P("shot", "sub"),
            P(None, "shot", "sub"),
            P("shot", "sub", None),
            P("shot", "sub"),
        ),
        out_specs=(
            P("shot", "sub"),
            P("shot", "sub"),
            P(("shot", "sub")),
        ),
        check_vma=False,
    )
```
